128 devices in a mesh: batch: 16 (over y, z), tensor: 8 (over x, core).
Axes of the slice: x: 4, y: 4, z: 4, core: 2. Of those that a mesh axis runs over, the one named last changes fastest.
Arguments:
- layer_input: bfloat16 [2, 192, 12288], P(None, None, 'batch'), may hold values from -100 to 100
- attn_gain: bfloat16 [12288], P('batch'), may hold values from 0.099609375 to 1.8984375
- ffn_gain: bfloat16 [12288], P('batch'), may hold values from 0.099609375 to 1.8984375
- query_weight: bfloat16 [12288, 12288], P('batch', 'tensor'), may hold values from -0.0546875 to 0.0546875
- keyval_weight: bfloat16 [2, 12288, 1024], P(None, 'batch', 'tensor'), may hold values from -0.0546875 to 0.0546875
- output_weight: bfloat16 [12288, 12288], P('tensor', 'batch'), may hold values from -0.0546875 to 0.0546875
- gateup_weight: bfloat16 [2, 12288, 21504], P(None, 'batch', 'tensor'), may hold values from -0.0546875 to 0.0546875
- down_weight: bfloat16 [21504, 12288], P('tensor', 'batch'), may hold values from -0.0390625 to 0.0390625
- past_cache: bfloat16 [2, 192, 256, 1024], P(None, 'batch', None, 'tensor'), may hold values from -103 to 103
- parent_rows: int32 [2, 192], replicated, may hold values from 0 to 191, as said below
Outputs:
- layer_out: bfloat16 [2, 192, 12288], P(None, 'tensor', 'batch')
- cache_out: bfloat16 [2, 192, 256, 1024], P(None, 'batch', None, 'tensor')
- fresh_out: bfloat16 [2, 192, 2, 1024], P(None, 'batch', None, 'tensor')
The draws below stay inside these ranges and needn't reach their ends.
Inputs may be any that keep to these rules, and one draw needn't show every extreme that they name: `parent_rows`: rows of one batch index are 12 consecutive rows. At every step, each batch index's child rows continue rows held by exactly 6 batch indices, exactly 2 child rows for each of them, in no fixed order among the child rows; a parent row may have any number of children.
All inputs are finite; a program needn't handle non-finite values.
Results may differ from the reference program's by a relative error of at most 0.0088.
Values may be sent and summed in bfloat16 or wider, within the bound.
No kernel may reach another device: no remote copies, remote signals or barrier semaphores. Data moves between devices by JAX's collectives and lax.ppermute only.
A program may use at most 128 MiB of HBM per device.

```python
import math
import jax
import jax.numpy as jnp
from jax import lax

D = 12288
HQ = 96
KVH = 8
HD = 128
FF = 21504
ROWS_DEV = 12
L = 256
SLOTS = 2
STEPS = 2
ROWS = 192


def draw_layer_input(key, part):
    key = jax.random.fold_in(key, 11)
    first_key, second_key = jax.random.split(key, 2)
    columns = jnp.arange(D, dtype=jnp.float32) / D
    rough = jnp.exp(jax.random.uniform(second_key, (D,), jnp.float32, -0.35, 0.35))
    column_scale = jnp.power(10.0, columns - 0.5) * rough
    values = jnp.clip(jax.random.normal(first_key, (STEPS, ROWS, D), jnp.float32), -6.0, 6.0) * column_scale
    return values.astype(jnp.bfloat16)


def draw_past_cache(key, part):
    key = jax.random.fold_in(key, 13)
    first_key = jax.random.fold_in(key, 0)
    shape = (2, ROWS, L, KVH * HD)
    values = jnp.clip(jax.random.normal(first_key, shape, jnp.float32), -6.0, 6.0)
    return values.astype(jnp.bfloat16)


def draw_parent_rows(key, part):
    key = jax.random.fold_in(key, 17)
    groups = ROWS // ROWS_DEV
    step_keys = jax.random.split(key, STEPS)

    def one_step(step_key):
        hot_key, shift_key, row_key, order_key = jax.random.split(step_key, 4)
        hottest = jax.random.randint(hot_key, (), 0, groups)
        shifts = jax.random.randint(shift_key, (groups,), 0, 4)
        offsets = jnp.arange(ROWS_DEV, dtype=jnp.int32) // SLOTS
        owners = (hottest + shifts[:, None] + offsets[None, :]) % groups
        picks = jax.random.randint(row_key, (groups, ROWS_DEV), 0, ROWS_DEV)
        orders = jax.vmap(lambda sub_key: jax.random.permutation(sub_key, ROWS_DEV))(jax.random.split(order_key, groups))
        owners = jnp.take_along_axis(owners, orders, axis=1)
        return (owners * ROWS_DEV + picks).reshape(ROWS).astype(jnp.int32)
    return jax.vmap(one_step)(step_keys)


def levels(own_key, dims, shards, low, high):
    def one(axis_at, blocks):
        steps = jax.random.uniform(jax.random.fold_in(jax.random.fold_in(own_key, 6), axis_at), (blocks,), jnp.float32, low / len(shards), high / len(shards))
        return jnp.repeat(jnp.exp(steps), dims[axis_at] // blocks).reshape((-1,) + (1,) * (len(dims) - axis_at - 1))

    level = one(*shards[0])
    for cut in shards[1:]:
        level = level * one(*cut)
    return level


def scatter_about(own_key, extent, scale, reach, cuts=(), kind=jnp.bfloat16):
    entries = scale * jax.random.normal(own_key, extent, jnp.float32)
    if cuts:
        entries = entries * levels(own_key, extent, cuts, -0.22, 0.18)
    return jnp.clip(entries, -reach, reach).astype(kind)


def setup_inputs(seed: int = 0) -> dict:
    key_list = jax.random.split(jax.random.key(seed), 11)
    return {
        "layer_input": draw_layer_input(jax.random.fold_in(key_list[10], 71), 0),
        "attn_gain": jnp.clip(1.0 + 0.18 * jax.random.normal(key_list[1], (D,), jnp.float32), 0.099609375, 1.8984375).astype(jnp.bfloat16),
        "ffn_gain": jnp.clip(1.0 + 0.18 * jax.random.normal(key_list[2], (D,), jnp.float32), 0.099609375, 1.8984375).astype(jnp.bfloat16),
        "query_weight": scatter_about(key_list[3], (D, HQ * HD), D ** -0.5, 0.0546875, ((0, 16), (1, 8))),
        "keyval_weight": scatter_about(key_list[4], (2, D, KVH * HD), D ** -0.5, 0.0546875, ((1, 16), (2, 8))),
        "output_weight": scatter_about(key_list[5], (HQ * HD, D), (HQ * HD) ** -0.5, 0.0546875, ((0, 8), (1, 16))),
        "gateup_weight": scatter_about(key_list[6], (2, D, FF), D ** -0.5, 0.0546875, ((1, 16), (2, 8))),
        "down_weight": scatter_about(key_list[7], (FF, D), FF ** -0.5, 0.0390625, ((0, 8), (1, 16))),
        "past_cache": draw_past_cache(jax.random.fold_in(key_list[10], 71), 0),
        "parent_rows": draw_parent_rows(jax.random.fold_in(key_list[10], 71), 0),
    }


rope_base = 1000000.0
norm_eps = 1e-05

def normalize(values, gain):
    mean_square = lax.optimization_barrier(jnp.mean(values * values, axis=-1, keepdims=True))
    return values * lax.rsqrt(mean_square + norm_eps) * gain.astype(jnp.float32)

def rotate(values, position, head_count):
    row_total = values.shape[0]
    shaped = values.reshape(row_total, head_count, HD)
    half_dim = HD // 2
    inverse = jnp.exp(-math.log(rope_base) * jnp.arange(half_dim, dtype=jnp.float32) * (2.0 / HD))
    angles = position * inverse
    cosine = jnp.cos(angles)
    sines = jnp.sin(angles)
    first_half = shaped[..., :half_dim]
    second_half = shaped[..., half_dim:]
    turned = jnp.concatenate([first_half * cosine - second_half * sines, second_half * cosine + first_half * sines], axis=-1)
    return turned.reshape(row_total, head_count * HD)

def attend_row(operands):
    query_row, key_row, value_row = operands
    group_size = HQ // KVH
    positions = key_row.shape[0]
    query_heads = query_row.astype(jnp.float32).reshape(KVH, group_size, HD)
    key_heads = key_row.astype(jnp.float32).reshape(positions, KVH, HD)
    value_heads = value_row.astype(jnp.float32).reshape(positions, KVH, HD)
    scores = jnp.einsum('kgd,tkd->kgt', query_heads, key_heads) * (1.0 / math.sqrt(HD))
    weights = jax.nn.softmax(scores, axis=-1).astype(jnp.bfloat16)
    weights = lax.optimization_barrier(weights).astype(jnp.float32)
    mixed = jnp.einsum('kgt,tkd->kgd', weights, value_heads)
    return mixed.astype(jnp.bfloat16).reshape(HQ * HD)

def reference(layer_input, attn_gain, ffn_gain, query_weight, keyval_weight, output_weight, gateup_weight, down_weight, past_cache, parent_rows):
    caches = jnp.concatenate([past_cache, jnp.zeros((2, ROWS, STEPS, KVH * HD), jnp.bfloat16)], axis=2)
    outputs = []
    for step_index in range(STEPS):
        position = L + step_index
        inputs = layer_input[step_index].astype(jnp.float32)
        normed = normalize(inputs, attn_gain).astype(jnp.bfloat16)
        queries = rotate(jnp.dot(normed, query_weight, preferred_element_type=jnp.float32), position, HQ).astype(jnp.bfloat16)
        new_keys = rotate(jnp.dot(normed, keyval_weight[0], preferred_element_type=jnp.float32), position, KVH).astype(jnp.bfloat16)
        new_values = jnp.dot(normed, keyval_weight[1], preferred_element_type=jnp.float32).astype(jnp.bfloat16)
        caches = jnp.take(caches, parent_rows[step_index].astype(jnp.int32), axis=1)
        caches = caches.at[:, :, position].set(jnp.stack([new_keys, new_values]))
        used_pages = caches[:, :, :position + 1]
        attended = lax.map(attend_row, (queries, used_pages[0], used_pages[1]))
        residual = inputs + jnp.dot(attended, output_weight, preferred_element_type=jnp.float32)
        hidden_in = normalize(residual, ffn_gain).astype(jnp.bfloat16)
        gate_sum = jnp.dot(hidden_in, gateup_weight[0], preferred_element_type=jnp.float32)
        up_sum = jnp.dot(hidden_in, gateup_weight[1], preferred_element_type=jnp.float32)
        activated = (jax.nn.silu(gate_sum) * up_sum).astype(jnp.bfloat16)
        down_sum = jnp.dot(activated, down_weight, preferred_element_type=jnp.float32)
        outputs.append((residual + down_sum).astype(jnp.bfloat16))
    return (jnp.stack(outputs), caches[:, :, :L], caches[:, :, L:])
```

```python
import functools
import math

import jax
import jax.numpy as jnp
from jax import lax
from jax.experimental import pallas as pl
from jax.experimental.pallas import tpu as pltpu
from jax.sharding import PartitionSpec as P

HD = 128
LANES = 128
STEPS = 2

rope_base = 1000000.0
norm_eps = 1e-05


def exchange(blocks, axis):
    return lax.all_to_all(blocks, axis, split_axis=0, concat_axis=0, tiled=True)


def gather_all(block, axis):
    copies = jnp.broadcast_to(block[None], (lax.axis_size(axis),) + block.shape)
    return exchange(lax.optimization_barrier(copies), axis)


def split_pair(values):
    high = values.astype(jnp.bfloat16)
    low = (values - high.astype(jnp.float32)).astype(jnp.bfloat16)
    return high, low


def rotary(steps, first_position):
    inverse = jnp.exp(
        -math.log(rope_base) * jnp.arange(HD // 2, dtype=jnp.float32) * (2.0 / HD)
    )
    angles = (first_position + steps).astype(jnp.float32)[:, None] * inverse[None, :]
    cosine, sine = jnp.cos(angles), jnp.sin(angles)
    return jnp.concatenate([cosine, cosine], axis=1), jnp.concatenate([-sine, sine], axis=1)


def rotate(heads, cosine, sine):
    swapped = jnp.concatenate([heads[..., HD // 2 :], heads[..., : HD // 2]], axis=-1)
    return heads * cosine + swapped * sine


def pick_kernel(index_ref, table_ref, out_ref):
    def body(row, carry):
        out_ref[row] = table_ref[index_ref[row]]
        return carry

    lax.fori_loop(0, out_ref.shape[0], body, 0, unroll=8)


def pick_rows(table, index):
    return pl.pallas_call(
        pick_kernel,
        out_shape=jax.ShapeDtypeStruct((index.shape[0],) + table.shape[1:], table.dtype),
        in_specs=[
            pl.BlockSpec(memory_space=pltpu.SMEM),
            pl.BlockSpec(memory_space=pltpu.VMEM),
        ],
        out_specs=pl.BlockSpec(memory_space=pltpu.VMEM),
        compiler_params=pltpu.CompilerParams(vmem_limit_bytes=32 * 1024 * 1024),
        cost_estimate=pl.CostEstimate(
            flops=0, bytes_accessed=3 * index.shape[0] * table[0].size, transcendentals=0
        ),
        name="pick_rows",
    )(index, table)


def on_device(
    layer_input,
    attn_gain,
    ffn_gain,
    query_weight,
    keyval_weight,
    output_weight,
    gateup_weight,
    down_weight,
    past_cache,
    parent_rows,
):
    batches = lax.axis_size("batch")
    tensors = lax.axis_size("tensor")
    tensor_index = lax.axis_index("tensor")
    _, rows, past, kv_width = past_cache.shape
    width = layer_input.shape[2]
    model = width * batches
    head_width = query_weight.shape[1]
    heads = head_width // HD
    hidden = gateup_weight.shape[2]
    both = STEPS * rows
    total = batches * both
    share = total // tensors
    span = past // batches

    parents = parent_rows.reshape(STEPS, batches, rows)
    origin = jnp.take(parent_rows[0], parent_rows[1], axis=0)
    wanted = jnp.stack([parents[0], origin.reshape(batches, rows)], axis=1).reshape(total)

    with jax.named_scope("cache_spread"):
        pieces = past_cache.reshape(2, rows, batches, span, kv_width).transpose(2, 1, 0, 3, 4)
        spread = exchange(pieces, "batch").reshape(batches * rows, 2, span, kv_width)

    with jax.named_scope("project"):
        inputs = (
            layer_input.reshape(STEPS, batches, rows, width)
            .transpose(1, 0, 2, 3)
            .reshape(total, width)
        )
        wide = inputs.astype(jnp.float32)
        squares = jnp.sum(wide * wide, axis=1)
        scaled = (wide * attn_gain.astype(jnp.float32)).astype(jnp.bfloat16)
        chosen = (
            parent_rows[1][:, None] == jnp.arange(batches * rows, dtype=jnp.int32)[None, :]
        ).astype(jnp.bfloat16)
        first_step = scaled.reshape(batches, STEPS, rows, width)[:, 0].reshape(-1, width)
        parent_scaled = jnp.dot(
            chosen, first_step, preferred_element_type=jnp.float32
        ).astype(jnp.bfloat16)
        parent_squares = jnp.dot(
            chosen.astype(jnp.float32),
            squares.reshape(batches, STEPS, rows)[:, 0].reshape(-1),
            precision=lax.Precision.HIGHEST,
        )
        project = functools.partial(jnp.dot, preferred_element_type=jnp.float32)
        parent_pair = jnp.stack(
            [
                project(parent_scaled, keyval_weight[0]).reshape(batches, rows, kv_width),
                project(parent_scaled, keyval_weight[1]).reshape(batches, rows, kv_width),
            ],
            axis=1,
        ).reshape(total, kv_width)
        parent_squares = jnp.concatenate(
            [parent_squares.reshape(batches, 1, rows)] * STEPS, axis=1
        ).reshape(total)
        statistics = jnp.stack(split_pair(squares) + split_pair(parent_squares), axis=1)
        sums = jnp.concatenate(
            [
                project(scaled, query_weight).astype(jnp.bfloat16),
                project(scaled, keyval_weight[0]).astype(jnp.bfloat16),
                project(scaled, keyval_weight[1]).astype(jnp.bfloat16),
                parent_pair.astype(jnp.bfloat16),
                jnp.pad(statistics, ((0, 0), (0, LANES - statistics.shape[1]))),
            ],
            axis=1,
        ).reshape(batches, both, -1)
        summed = jnp.sum(exchange(sums, "batch").astype(jnp.float32), axis=0)

    with jax.named_scope("cache_return"):
        picked = pick_rows(spread, wanted).reshape(batches, both, 2, span, kv_width)
        returned = exchange(picked, "batch").transpose(2, 1, 0, 3, 4)
        caches = returned.reshape(2, both, past, kv_width)
        cache_out = caches[:, rows:]

    with jax.named_scope("attention"):
        edge = head_width + 3 * kv_width
        mean = (summed[:, edge] + summed[:, edge + 1]) / model
        parent_mean = (summed[:, edge + 2] + summed[:, edge + 3]) / model
        scale = lax.rsqrt(mean + norm_eps)[:, None]
        parent_scale = lax.rsqrt(parent_mean + norm_eps)[:, None]
        step_of = jnp.arange(both, dtype=jnp.int32) // rows
        cosine, sine = rotary(step_of, past)
        queries = rotate(
            (summed[:, :head_width] * scale).reshape(both, heads, HD),
            cosine[:, None],
            sine[:, None],
        ).astype(jnp.bfloat16)
        new_keys = rotate(
            summed[:, head_width : head_width + kv_width] * scale, cosine, sine
        ).astype(jnp.bfloat16)
        new_values = (
            summed[:, head_width + kv_width : head_width + 2 * kv_width] * scale
        ).astype(jnp.bfloat16)
        parent_sums = summed[:, head_width + 2 * kv_width : edge] * parent_scale
        parent_keys = rotate(parent_sums[:rows], cosine[:rows], sine[:rows]).astype(jnp.bfloat16)
        parent_values = parent_sums[rows:].astype(jnp.bfloat16)
        fresh_keys = jnp.stack(
            [jnp.concatenate([new_keys[:rows], parent_keys]), new_keys], axis=1
        )
        fresh_values = jnp.stack(
            [jnp.concatenate([new_values[:rows], parent_values]), new_values], axis=1
        )
        fresh_out = jnp.stack([fresh_keys[rows:], fresh_values[rows:]])
        old_scores = jnp.einsum(
            "ngd,ntd->ngt", queries, caches[0], preferred_element_type=jnp.float32
        )
        fresh_scores = jnp.einsum(
            "ngd,ntd->ngt", queries, fresh_keys, preferred_element_type=jnp.float32
        )
        scores = jnp.concatenate([old_scores, fresh_scores], axis=2) * (1.0 / math.sqrt(HD))
        place = jnp.arange(past + STEPS, dtype=jnp.int32)
        seen = place[None, :] <= (past + step_of)[:, None]
        scores = jnp.where(seen[:, None, :], scores, -jnp.inf)
        weights = jax.nn.softmax(scores, axis=-1).astype(jnp.bfloat16)
        attended = jnp.einsum(
            "ngt,ntd->ngd", weights[..., :past], caches[1], preferred_element_type=jnp.float32
        ) + jnp.einsum(
            "ngt,ntd->ngd", weights[..., past:], fresh_values, preferred_element_type=jnp.float32
        )
        attended = attended.astype(jnp.bfloat16).reshape(both, head_width)
        attended = gather_all(attended, "batch").reshape(total, head_width)

    with jax.named_scope("output_projection"):
        mixed = jnp.dot(attended, output_weight, preferred_element_type=jnp.float32)
        mixed = exchange(mixed.astype(jnp.bfloat16).reshape(tensors, share, width), "tensor")
        own_inputs = lax.dynamic_slice_in_dim(inputs, tensor_index * share, share, 0)
        residual = own_inputs.astype(jnp.float32) + jnp.sum(mixed.astype(jnp.float32), axis=0)
        gain = ffn_gain.astype(jnp.float32)
        lifted = gather_all((residual * gain).astype(jnp.bfloat16), "tensor")
        lifted = lifted.reshape(total, width)

    with jax.named_scope("gate_up"):
        plain = lifted.astype(jnp.float32) * (1.0 / gain)
        squares = jnp.stack(split_pair(jnp.sum(plain * plain, axis=1)), axis=1)
        sums = jnp.concatenate(
            [
                project(lifted, gateup_weight[0]).astype(jnp.bfloat16),
                project(lifted, gateup_weight[1]).astype(jnp.bfloat16),
                jnp.pad(squares, ((0, 0), (0, LANES - squares.shape[1]))),
            ],
            axis=1,
        ).reshape(batches, both, -1)
        summed = jnp.sum(exchange(sums, "batch").astype(jnp.float32), axis=0)
        mean = (summed[:, 2 * hidden] + summed[:, 2 * hidden + 1]) / model
        summed = summed[:, : 2 * hidden] * lax.rsqrt(mean + norm_eps)[:, None]
        activated = (jax.nn.silu(summed[:, :hidden]) * summed[:, hidden:]).astype(jnp.bfloat16)
        activated = gather_all(activated, "batch").reshape(total, hidden)

    with jax.named_scope("down_projection"):
        lowered = jnp.dot(activated, down_weight, preferred_element_type=jnp.float32)
        lowered = exchange(lowered.astype(jnp.bfloat16).reshape(tensors, share, width), "tensor")
        final = (residual + jnp.sum(lowered.astype(jnp.float32), axis=0)).astype(jnp.bfloat16)
        layer_out = (
            final.reshape(share // both, STEPS, rows, width)
            .transpose(1, 0, 2, 3)
            .reshape(STEPS, share // STEPS, width)
        )
    return layer_out, cache_out, fresh_out


def solution(mesh):
    return jax.shard_map(
        on_device,
        mesh=mesh,
        in_specs=(
            P(None, None, "batch"),
            P("batch"),
            P("batch"),
            P("batch", "tensor"),
            P(None, "batch", "tensor"),
            P("tensor", "batch"),
            P(None, "batch", "tensor"),
            P("tensor", "batch"),
            P(None, "batch", None, "tensor"),
            P(),
        ),
        out_specs=(
            P(None, "tensor", "batch"),
            P(None, "batch", None, "tensor"),
            P(None, "batch", None, "tensor"),
        ),
        check_vma=False,
    )
```

```python
import functools
import math

import jax
import jax.numpy as jnp
from jax import lax
from jax.experimental import pallas as pl
from jax.experimental.pallas import tpu as pltpu
from jax.sharding import PartitionSpec as P

HD = 128
LANES = 128
STEPS = 2
MIB = 1024 * 1024

rope_base = 1000000.0
norm_eps = 1e-05


def exchange(blocks, axis):
    return lax.all_to_all(blocks, axis, split_axis=0, concat_axis=0, tiled=True)


def gather_all(block, axis):
    copies = jnp.broadcast_to(block[None], (lax.axis_size(axis),) + block.shape)
    gathered = exchange(lax.optimization_barrier(copies), axis)
    return gathered.reshape((-1,) + block.shape[1:])


def after(value, earlier):
    return lax.optimization_barrier((value, earlier))[0]


def shift_along(block, minor_axis, count):
    side = math.isqrt(lax.axis_size("batch"))
    pairs = []
    for major in range(side):
        for minor in range(side):
            target = (
                (major, (minor + count) % side) if minor_axis else ((major + count) % side, minor)
            )
            pairs.append((major * side + minor, target[0] * side + target[1]))
    return lax.ppermute(block, "batch", pairs)


def shift_chips(block, count):
    size = lax.axis_size("tensor")
    return lax.ppermute(block, "tensor", [(at, (at + 2 * count) % size) for at in range(size)])


def swap_cores(block):
    size = lax.axis_size("tensor")
    return lax.ppermute(block, "tensor", [(at, at ^ 1) for at in range(size)])


def shift_both(first, second, first_minor):
    side = len(first)
    middle = side // 2
    others = [count for count in range(1, side) if count != middle]
    first_moved, second_moved = {0: first[0]}, {0: second[0]}
    for count in others + [middle]:
        first_moved[count] = shift_along(first[count], first_minor, count)
    for count in others:
        second_moved[count] = shift_along(second[count], 1 - first_minor, count)
    second_moved[middle] = shift_along(
        after(second[middle], second_moved[1]), 1 - first_minor, middle
    )
    return [first_moved[at] for at in range(side)], [second_moved[at] for at in range(side)]


def fold_kernel(count, *refs):
    sources, targets = refs[:count], refs[count:]
    terms = []
    for source in sources:
        terms += [source] if len(source.shape) == 2 else [source.at[at] for at in range(source.shape[0])]
    total = terms[0][...].astype(jnp.float32)
    for term in terms[1:]:
        total = total + term[...].astype(jnp.float32)
    rows = total.shape[0] // len(targets)
    for place, target in enumerate(targets):
        target[...] = total[place * rows : (place + 1) * rows].astype(target.dtype)


def fold(sources, pieces):
    rows, columns = sources[0].shape[-2:]
    kinds = [jnp.float32] + [jnp.bfloat16] * (pieces - 1)
    whole = pl.BlockSpec(memory_space=pltpu.VMEM)
    return pl.pallas_call(
        functools.partial(fold_kernel, len(sources)),
        out_shape=[jax.ShapeDtypeStruct((rows // pieces, columns), kind) for kind in kinds],
        in_specs=[whole] * len(sources),
        out_specs=[whole] * pieces,
        compiler_params=pltpu.CompilerParams(vmem_limit_bytes=32 * MIB),
        cost_estimate=pl.CostEstimate(flops=1, bytes_accessed=1, transcendentals=0),
        name="fold",
    )(*sources)


def add_over_batch(first, second, earlier):
    side = len(first)
    first, second = shift_both(first, second, 1)
    first, second = after((first, second), earlier)
    first, second = fold(first, side), fold(second, side)
    first, second = shift_both(first, second, 0)
    return [functools.reduce(lambda a, b: a + b.astype(jnp.float32), own) for own in (first, second)]


def exchange_minor(blocks):
    side = math.isqrt(lax.axis_size("batch"))
    groups = [[major * side + minor for minor in range(side)] for major in range(side)]
    return lax.all_to_all(
        blocks, "batch", split_axis=0, concat_axis=0, tiled=True, axis_index_groups=groups
    )


def add_along(own, terms):
    return functools.reduce(lambda total, term: total + term.astype(jnp.float32), terms, own)


def add_crossed(first, second):
    side = len(second)
    others = range(1, side)
    moved = [second[0]] + [shift_along(second[count], 0, count) for count in others]
    arrived = exchange_minor(first)
    summed = fold([arrived], side)
    first = add_along(summed[0], [shift_along(summed[count], 0, count) for count in others])
    crossed = add_along(moved[0].astype(jnp.float32), moved[1:]).astype(jnp.bfloat16)
    crossed = exchange_minor(crossed.reshape((side, -1) + crossed.shape[1:]))
    return first, jnp.sum(crossed.astype(jnp.float32), axis=0)


def add_over_tensor(kept, sent):
    chips = lax.axis_size("tensor") // 2
    pieces = fold([kept, swap_cores(sent)], chips)
    total = pieces[0]
    for count in range(1, chips):
        total = total + shift_chips(pieces[count], count).astype(jnp.float32)
    return total


def blocks_along(values, side, place):
    rows = values.shape[0] // (side * side)
    return jnp.concatenate(
        [
            values[(major * side + place) * rows : (major * side + place + 1) * rows]
            for major in range(side)
        ],
        axis=0,
    )


def one_hot(index, count):
    places = lax.broadcasted_iota(jnp.int32, (index.shape[0], count), 1)
    return jnp.where(places == index, 1.0, 0.0).astype(jnp.bfloat16)


def dot(left, right):
    return jnp.dot(left, right, preferred_element_type=jnp.float32)


def split_pair(values):
    high = values.astype(jnp.bfloat16).astype(jnp.float32)
    return [high, values - high]


def in_lanes(columns):
    lanes = lax.broadcasted_iota(jnp.int32, (columns[0].shape[0], LANES), 1)
    packed = jnp.zeros(lanes.shape, jnp.float32)
    for place, value in enumerate(columns):
        packed = jnp.where(lanes == place, value, packed)
    return packed


def project_kernel(
    side, order_ref, parent_ref, input_ref, gain_ref, query_ref, keyval_ref, *out_refs
):
    steps, count, width = input_ref.shape
    source = input_ref[...].reshape(steps * count, width)
    gain = gain_ref[...].astype(jnp.float32)
    order = order_ref[...]
    is_key = order < count
    own = dot(one_hot(order, steps * count), source)
    parents = dot(one_hot(parent_ref[...], count), input_ref[0]).astype(jnp.bfloat16)
    parents = dot(one_hot(jnp.where(is_key, order, order - count), count), parents)
    statistics = split_pair(jnp.sum(own * own, axis=1, keepdims=True)) + split_pair(
        jnp.sum(parents * parents, axis=1, keepdims=True)
    )
    own = (own * gain).astype(jnp.bfloat16)
    parents = (parents * gain).astype(jnp.bfloat16)
    values = jnp.concatenate(
        [
            dot(own, query_ref[...]),
            dot(own, keyval_ref[0]),
            dot(own, keyval_ref[1]),
            jnp.where(is_key, dot(parents, keyval_ref[0]), dot(parents, keyval_ref[1])),
            in_lanes(statistics),
        ],
        axis=1,
    ).astype(jnp.float32)
    half = values.shape[1] // 2
    rows = values.shape[0] // side
    for place in range(side):
        out_refs[place][...] = blocks_along(values[:, :half], side, place).astype(jnp.bfloat16)
        out_refs[side + place][...] = values[place * rows : (place + 1) * rows, half:].astype(
            jnp.bfloat16
        )


def project_rows(side, order, parents, layer_input, gain, query_weight, keyval_weight):
    total = order.shape[0]
    columns = query_weight.shape[1] + 3 * keyval_weight.shape[2] + LANES
    block = jax.ShapeDtypeStruct((total // side, columns // 2), jnp.bfloat16)
    whole = pl.BlockSpec(memory_space=pltpu.VMEM)
    return pl.pallas_call(
        functools.partial(project_kernel, side),
        out_shape=[block] * (2 * side),
        in_specs=[whole] * 6,
        out_specs=[whole] * (2 * side),
        compiler_params=pltpu.CompilerParams(vmem_limit_bytes=48 * MIB),
        cost_estimate=pl.CostEstimate(
            flops=2 * total * columns * gain.shape[0],
            bytes_accessed=2 * (gain.shape[0] + total) * columns,
            transcendentals=0,
        ),
        name="project_rows",
    )(order, parents, layer_input, gain.reshape(1, -1), query_weight, keyval_weight)


def gate_up_kernel(side, tile, order_ref, near_ref, far_ref, gain_ref, weight_ref, *out_refs):
    first_ref, second_refs = out_refs[0], out_refs[1:]
    lifted = jnp.concatenate([near_ref[...], far_ref[...]], axis=0)
    ordered = dot(one_hot(order_ref[...], lifted.shape[0]), lifted)
    plain = ordered * (1.0 / gain_ref[...].astype(jnp.float32))
    statistics = in_lanes(split_pair(jnp.sum(plain * plain, axis=1, keepdims=True)))
    ordered = ordered.astype(jnp.bfloat16)
    hidden = weight_ref.shape[2]
    rows = ordered.shape[0] // side
    for place in range(side):
        first_ref[place, :, hidden:] = blocks_along(statistics, side, place).astype(jnp.bfloat16)

    def one_tile(columns):
        gates = dot(ordered, weight_ref[0, :, columns])
        for place in range(side):
            first_ref[place, :, columns] = blocks_along(gates, side, place).astype(jnp.bfloat16)
        ups = dot(ordered, weight_ref[1, :, columns])
        for place in range(side):
            second_refs[place][:, columns] = ups[place * rows : (place + 1) * rows].astype(
                jnp.bfloat16
            )

    @pl.loop(0, hidden // tile)
    def _(step):
        one_tile(pl.ds(pl.multiple_of(step * tile, LANES), tile))

    if hidden % tile:
        one_tile(pl.ds(hidden // tile * tile, hidden % tile))


def gate_up(side, order, near, far, gain, weight, tile):
    total, width = order.shape[0], near.shape[1]
    hidden = weight.shape[2]
    whole = pl.BlockSpec(memory_space=pltpu.VMEM)
    return pl.pallas_call(
        functools.partial(gate_up_kernel, side, tile),
        out_shape=[jax.ShapeDtypeStruct((side, total // side, hidden + LANES), jnp.bfloat16)]
        + [jax.ShapeDtypeStruct((total // side, hidden), jnp.bfloat16)] * side,
        in_specs=[whole] * 5,
        out_specs=[whole] * (1 + side),
        compiler_params=pltpu.CompilerParams(vmem_limit_bytes=48 * MIB),
        cost_estimate=pl.CostEstimate(
            flops=4 * total * width * hidden,
            bytes_accessed=4 * hidden * (width + total),
            transcendentals=0,
        ),
        name="gate_up",
    )(order, near, far, gain.reshape(1, -1), weight)


def spread_dot_kernel(place_ref, rows_ref, weight_ref, kept_ref, sent_ref, total_ref):
    values = dot(rows_ref[...], weight_ref[...])
    blocks = place_ref.shape[0]
    rows = values.shape[0] // blocks
    for at in range(blocks):
        target = pl.ds(pl.multiple_of(place_ref[at], 8), rows)
        total_ref[target, :] = values[at * rows : (at + 1) * rows]
    half = kept_ref.shape[0]
    kept_ref[...] = total_ref[:half]
    sent_ref[...] = total_ref[half:]


def spread_dot(places, values, weight):
    total, width = values.shape[0], weight.shape[1]
    whole = pl.BlockSpec(memory_space=pltpu.VMEM)
    return pl.pallas_call(
        spread_dot_kernel,
        out_shape=[jax.ShapeDtypeStruct((total // 2, width), jnp.float32)] * 2,
        in_specs=[pl.BlockSpec(memory_space=pltpu.SMEM), whole, whole],
        out_specs=[whole] * 2,
        scratch_shapes=[pltpu.VMEM((total, width), jnp.float32)],
        compiler_params=pltpu.CompilerParams(vmem_limit_bytes=48 * MIB),
        cost_estimate=pl.CostEstimate(
            flops=2 * total * weight.size,
            bytes_accessed=2 * weight.size + 2 * total * (weight.shape[0] + 4 * width),
            transcendentals=0,
        ),
        name="spread_dot",
    )(places, values, weight)


def rotary(steps, first_position):
    inverse = jnp.exp(
        -math.log(rope_base) * jnp.arange(HD // 2, dtype=jnp.float32) * (2.0 / HD)
    )
    angles = (first_position + steps).astype(jnp.float32)[:, None] * inverse[None, :]
    cosine, sine = jnp.cos(angles), jnp.sin(angles)
    return jnp.concatenate([cosine, cosine], axis=1), jnp.concatenate([-sine, sine], axis=1)


def rotate(heads, cosine, sine):
    swapped = jnp.concatenate([heads[..., HD // 2 :], heads[..., : HD // 2]], axis=-1)
    return heads * cosine + swapped * sine


def pick_kernel(index_ref, table_ref, out_ref):
    def body(row, carry):
        out_ref[row] = table_ref[index_ref[row]]
        return carry

    lax.fori_loop(0, out_ref.shape[0], body, 0, unroll=8)


def pick_rows(table, index):
    return pl.pallas_call(
        pick_kernel,
        out_shape=jax.ShapeDtypeStruct((index.shape[0],) + table.shape[1:], table.dtype),
        in_specs=[
            pl.BlockSpec(memory_space=pltpu.SMEM),
            pl.BlockSpec(memory_space=pltpu.VMEM),
        ],
        out_specs=pl.BlockSpec(memory_space=pltpu.VMEM),
        compiler_params=pltpu.CompilerParams(vmem_limit_bytes=32 * MIB),
        cost_estimate=pl.CostEstimate(
            flops=0, bytes_accessed=3 * index.shape[0] * table[0].size, transcendentals=0
        ),
        name="pick_rows",
    )(index, table)


def on_device(
    layer_input,
    attn_gain,
    ffn_gain,
    query_weight,
    keyval_weight,
    output_weight,
    gateup_weight,
    down_weight,
    past_cache,
    parent_rows,
):
    batches = lax.axis_size("batch")
    tensors = lax.axis_size("tensor")
    side = math.isqrt(batches)
    chips = tensors // 2
    batch_index = lax.axis_index("batch")
    tensor_index = lax.axis_index("tensor")
    my_major, my_minor = batch_index // side, batch_index % side
    my_chip, my_core = tensor_index // 2, tensor_index % 2
    _, rows, past, kv_width = past_cache.shape
    width = layer_input.shape[2]
    model = width * batches
    head_width = query_weight.shape[1]
    heads = head_width // HD
    hidden = gateup_weight.shape[2]
    both = STEPS * rows
    total = batches * both
    share = total // tensors
    span = past // batches

    with jax.named_scope("cache_spread"):
        pieces = past_cache.reshape(2, rows, batches, span, kv_width).transpose(2, 1, 0, 3, 4)
        spread = exchange(pieces, "batch").reshape(batches * rows, 2, span, kv_width)

    with jax.named_scope("places"):
        parents = parent_rows.reshape(STEPS, batches, rows)
        origin = jnp.take(parent_rows[0], parent_rows[1], axis=0)
        wanted = jnp.stack([parents[0], origin.reshape(batches, rows)], axis=1).reshape(total)
        place = jnp.arange(total, dtype=jnp.int32)
        inner = place % both
        ahead = (my_major + place // (side * both)) % side * side
        ahead = ahead + (my_minor + place // both) % side
        input_order = ((inner // rows) * (batches * rows) + ahead * rows + inner % rows)[:, None]
        row = (my_major + place // (side * both)) % side * side + place // both % side
        row = row * both + inner
        owner = row // share
        lifted_order = (owner % 2 != my_core).astype(jnp.int32) * (total // 2)
        lifted_order = lifted_order + (my_chip - owner // 2 + chips) % chips * share
        lifted_order = (lifted_order + row % share)[:, None]
        block = jnp.arange(batches, dtype=jnp.int32)
        owner = block * both // share
        targets = (owner % 2 != my_core).astype(jnp.int32) * (total // 2)
        targets = targets + (owner // 2 - my_chip + chips) % chips * share
        targets = targets + block * both % share

    with jax.named_scope("project"):
        blocks = project_rows(
            side,
            input_order,
            parent_rows[1][:, None],
            after(layer_input, pieces),
            attn_gain,
            query_weight,
            keyval_weight,
        )
        picked = pick_rows(spread, wanted).reshape(batches, both, 2, span, kv_width)
        summed = jnp.concatenate(add_over_batch(blocks[:side], blocks[side:], picked), axis=1)

    with jax.named_scope("cache_return"):
        returned = exchange(picked, "batch").transpose(2, 1, 0, 3, 4)
        caches = returned.reshape(2, both, past, kv_width)
        cache_out = caches[:, rows:]

    with jax.named_scope("attention"):
        edge = head_width + 3 * kv_width
        mean = (summed[:, edge] + summed[:, edge + 1]) / model
        parent_mean = (summed[:, edge + 2] + summed[:, edge + 3]) / model
        scale = lax.rsqrt(mean + norm_eps)[:, None]
        parent_scale = lax.rsqrt(parent_mean + norm_eps)[:, None]
        step_of = jnp.arange(both, dtype=jnp.int32) // rows
        cosine, sine = rotary(step_of, past)
        queries = rotate(
            (summed[:, :head_width] * scale).reshape(both, heads, HD),
            cosine[:, None],
            sine[:, None],
        ).astype(jnp.bfloat16)
        new_keys = rotate(
            summed[:, head_width : head_width + kv_width] * scale, cosine, sine
        ).astype(jnp.bfloat16)
        new_values = (
            summed[:, head_width + kv_width : head_width + 2 * kv_width] * scale
        ).astype(jnp.bfloat16)
        parent_sums = summed[:, head_width + 2 * kv_width : edge] * parent_scale
        parent_keys = rotate(parent_sums[:rows], cosine[:rows], sine[:rows]).astype(jnp.bfloat16)
        parent_values = parent_sums[rows:].astype(jnp.bfloat16)
        fresh_keys = jnp.stack(
            [jnp.concatenate([new_keys[:rows], parent_keys]), new_keys], axis=1
        )
        fresh_values = jnp.stack(
            [jnp.concatenate([new_values[:rows], parent_values]), new_values], axis=1
        )
        fresh_out = jnp.stack([fresh_keys[rows:], fresh_values[rows:]])
        old_scores = jnp.einsum(
            "ngd,ntd->ngt", queries, caches[0], preferred_element_type=jnp.float32
        )
        fresh_scores = jnp.einsum(
            "ngd,ntd->ngt", queries, fresh_keys, preferred_element_type=jnp.float32
        )
        scores = jnp.concatenate([old_scores, fresh_scores], axis=2) * (1.0 / math.sqrt(HD))
        position = jnp.arange(past + STEPS, dtype=jnp.int32)
        seen = position[None, :] <= (past + step_of)[:, None]
        scores = jnp.where(seen[:, None, :], scores, -jnp.inf)
        weights = jax.nn.softmax(scores, axis=-1).astype(jnp.bfloat16)
        attended = jnp.einsum(
            "ngt,ntd->ngd", weights[..., :past], caches[1], preferred_element_type=jnp.float32
        ) + jnp.einsum(
            "ngt,ntd->ngd", weights[..., past:], fresh_values, preferred_element_type=jnp.float32
        )
        attended = attended.astype(jnp.bfloat16).reshape(both, head_width)
        attended = gather_all(attended, "batch")

    with jax.named_scope("output_projection"):
        own_inputs = lax.dynamic_slice_in_dim(
            layer_input, tensor_index * (share // STEPS), share // STEPS, 1
        )
        own_inputs = (
            own_inputs.reshape(STEPS, share // both, rows, width)
            .transpose(1, 0, 2, 3)
            .reshape(share, width)
        )
        mixed = add_over_tensor(*spread_dot(targets, attended, output_weight))
        residual = own_inputs.astype(jnp.float32) + mixed
        lifted = (residual * ffn_gain.astype(jnp.float32)).astype(jnp.bfloat16)
        near = jnp.concatenate(
            [lifted] + [shift_chips(lifted, count) for count in range(1, chips)], axis=0
        )
        far = swap_cores(near)

    with jax.named_scope("gate_up"):
        blocks = gate_up(side, lifted_order, near, far, ffn_gain, gateup_weight, 768)
        gates, ups = add_crossed(blocks[0], blocks[1:])
        mean = (gates[:, hidden] + gates[:, hidden + 1]) / model
        scale = lax.rsqrt(mean + norm_eps)[:, None]
        gates, ups = gates[:, :hidden] * scale, ups * scale
        activated = (jax.nn.silu(gates) * ups).astype(jnp.bfloat16)
        activated = gather_all(activated, "batch")

    with jax.named_scope("down_projection"):
        lowered = add_over_tensor(*spread_dot(targets, activated, down_weight))
        final = (residual + lowered).astype(jnp.bfloat16)
        layer_out = (
            final.reshape(share // both, STEPS, rows, width)
            .transpose(1, 0, 2, 3)
            .reshape(STEPS, share // STEPS, width)
        )
    return layer_out, cache_out, fresh_out


def solution(mesh):
    return jax.shard_map(
        on_device,
        mesh=mesh,
        in_specs=(
            P(None, None, "batch"),
            P("batch"),
            P("batch"),
            P("batch", "tensor"),
            P(None, "batch", "tensor"),
            P("tensor", "batch"),
            P(None, "batch", "tensor"),
            P("tensor", "batch"),
            P(None, "batch", None, "tensor"),
            P(),
        ),
        out_specs=(
            P(None, "tensor", "batch"),
            P(None, "batch", None, "tensor"),
            P(None, "batch", None, "tensor"),
        ),
        check_vma=False,
    )
```

```python
import functools
import math

import jax
import jax.numpy as jnp
import numpy as np
from jax import lax
from jax.experimental import pallas as pl
from jax.experimental.pallas import tpu as pltpu
from jax.sharding import PartitionSpec as P

HD = 128
LANES = 128
STEPS = 2
MIB = 1024 * 1024

rope_base = 1000000.0
norm_eps = 1e-05


def exchange(blocks, axis):
    return lax.all_to_all(blocks, axis, split_axis=0, concat_axis=0, tiled=True)


def gather_all(block, axis):
    copies = jnp.broadcast_to(block[None], (lax.axis_size(axis),) + block.shape)
    gathered = exchange(lax.optimization_barrier(copies), axis)
    return gathered.reshape((-1,) + block.shape[1:])


def after(value, earlier):
    return lax.optimization_barrier((value, earlier))[0]


def shift_along(block, minor_axis, count):
    side = math.isqrt(lax.axis_size("batch"))
    pairs = []
    for major in range(side):
        for minor in range(side):
            target = (
                (major, (minor + count) % side) if minor_axis else ((major + count) % side, minor)
            )
            pairs.append((major * side + minor, target[0] * side + target[1]))
    return lax.ppermute(block, "batch", pairs)


def shift_chips(block, count):
    size = lax.axis_size("tensor")
    return lax.ppermute(block, "tensor", [(at, (at + 2 * count) % size) for at in range(size)])


def swap_cores(block):
    size = lax.axis_size("tensor")
    return lax.ppermute(block, "tensor", [(at, at ^ 1) for at in range(size)])


def fold_kernel(count, *refs):
    sources, targets = refs[:count], refs[count:]
    terms = []
    for source in sources:
        terms += [source] if len(source.shape) == 2 else [source.at[at] for at in range(source.shape[0])]
    total = terms[0][...].astype(jnp.float32)
    for term in terms[1:]:
        total = total + term[...].astype(jnp.float32)
    rows = total.shape[0] // len(targets)
    for place, target in enumerate(targets):
        target[...] = total[place * rows : (place + 1) * rows].astype(target.dtype)


def fold(sources, pieces):
    rows, columns = sources[0].shape[-2:]
    kinds = [jnp.float32] + [jnp.bfloat16] * (pieces - 1)
    whole = pl.BlockSpec(memory_space=pltpu.VMEM)
    return pl.pallas_call(
        functools.partial(fold_kernel, len(sources)),
        out_shape=[jax.ShapeDtypeStruct((rows // pieces, columns), kind) for kind in kinds],
        in_specs=[whole] * len(sources),
        out_specs=[whole] * pieces,
        compiler_params=pltpu.CompilerParams(vmem_limit_bytes=32 * MIB),
        cost_estimate=pl.CostEstimate(flops=1, bytes_accessed=1, transcendentals=0),
        name="fold",
    )(*sources)


def exchange_minor(blocks):
    side = math.isqrt(lax.axis_size("batch"))
    groups = [[major * side + minor for minor in range(side)] for major in range(side)]
    return lax.all_to_all(
        blocks, "batch", split_axis=0, concat_axis=0, tiled=True, axis_index_groups=groups
    )


def add_along(own, terms):
    return functools.reduce(lambda total, term: total + term.astype(jnp.float32), terms, own)


def add_crossed(first, second):
    side = len(second)
    others = range(1, side)
    moved = [second[0]] + [shift_along(second[count], 0, count) for count in others]
    arrived = exchange_minor(first)
    summed = fold([arrived], side)
    first = add_along(summed[0], [shift_along(summed[count], 0, count) for count in others])
    crossed = add_along(moved[0].astype(jnp.float32), moved[1:]).astype(jnp.bfloat16)
    crossed = exchange_minor(crossed.reshape((side, -1) + crossed.shape[1:]))
    return first, jnp.sum(crossed.astype(jnp.float32), axis=0)


def add_over_tensor(kept, sent):
    chips = lax.axis_size("tensor") // 2
    pieces = fold([kept, swap_cores(sent)], chips)
    total = pieces[0]
    for count in range(1, chips):
        total = total + shift_chips(pieces[count], count).astype(jnp.float32)
    return total


def blocks_along(values, side, place):
    rows = values.shape[0] // (side * side)
    return jnp.concatenate(
        [
            values[(major * side + place) * rows : (major * side + place + 1) * rows]
            for major in range(side)
        ],
        axis=0,
    )


def one_hot(index, count):
    places = lax.broadcasted_iota(jnp.int32, (index.shape[0], count), 1)
    return jnp.where(places == index, 1.0, 0.0).astype(jnp.bfloat16)


def dot(left, right):
    return jnp.dot(left, right, preferred_element_type=jnp.float32)


def split_pair(values):
    high = values.astype(jnp.bfloat16).astype(jnp.float32)
    return [high, values - high]


def in_lanes(columns):
    lanes = lax.broadcasted_iota(jnp.int32, (columns[0].shape[0], LANES), 1)
    packed = jnp.zeros(lanes.shape, jnp.float32)
    for place, value in enumerate(columns):
        packed = jnp.where(lanes == place, value, packed)
    return packed


def project_kernel(
    order_ref, parent_ref, input_ref, gain_ref, query_ref, keyval_ref, out_ref
):
    steps, count, width = input_ref.shape
    source = input_ref[...].reshape(steps * count, width)
    gain = gain_ref[...].astype(jnp.float32)
    order = order_ref[...]
    is_key = order < count
    own = dot(one_hot(order, steps * count), source)
    parents = dot(one_hot(parent_ref[...], count), input_ref[0]).astype(jnp.bfloat16)
    parents = dot(one_hot(jnp.where(is_key, order, order - count), count), parents)
    statistics = split_pair(jnp.sum(own * own, axis=1, keepdims=True)) + split_pair(
        jnp.sum(parents * parents, axis=1, keepdims=True)
    )
    own = (own * gain).astype(jnp.bfloat16)
    parents = (parents * gain).astype(jnp.bfloat16)
    values = jnp.concatenate(
        [
            dot(own, query_ref[...]),
            dot(own, keyval_ref[0]),
            dot(own, keyval_ref[1]),
            jnp.where(is_key, dot(parents, keyval_ref[0]), dot(parents, keyval_ref[1])),
            in_lanes(statistics),
        ],
        axis=1,
    ).astype(jnp.float32)
    blocks, held, _ = out_ref.shape
    rows = values.shape[0] // blocks
    for block in range(blocks):
        part = values[block * rows : (block + 1) * rows]
        for at in range(held // (2 * rows)):
            pair = [
                part[:, (2 * at + side) * LANES : (2 * at + side + 1) * LANES] for side in range(2)
            ]
            out_ref[block, 2 * at * rows : 2 * (at + 1) * rows] = jnp.concatenate(
                pair, axis=0
            ).astype(jnp.bfloat16)


def project_rows(batches, order, parents, layer_input, gain, query_weight, keyval_weight):
    total = order.shape[0]
    columns = query_weight.shape[1] + 3 * keyval_weight.shape[2] + LANES
    held = total // batches * columns // LANES
    whole = pl.BlockSpec(memory_space=pltpu.VMEM)
    return pl.pallas_call(
        project_kernel,
        out_shape=jax.ShapeDtypeStruct((batches, held, LANES), jnp.bfloat16),
        in_specs=[whole] * 6,
        out_specs=whole,
        compiler_params=pltpu.CompilerParams(vmem_limit_bytes=48 * MIB),
        cost_estimate=pl.CostEstimate(
            flops=2 * total * columns * gain.shape[0],
            bytes_accessed=2 * (gain.shape[0] + total) * columns,
            transcendentals=0,
        ),
        name="project_rows",
    )(order, parents, layer_input, gain.reshape(1, -1), query_weight, keyval_weight)


def gate_up_kernel(side, spans, order_ref, near_ref, far_ref, gain_ref, weight_ref, *refs):
    first_ref, second_refs = refs[0], refs[1 : 1 + side]
    held_ref, first_held, second_held, in_sems, first_sems, second_sems = refs[1 + side :]
    hidden = weight_ref.shape[2]
    loads = {}
    for half in (1, 0):
        for at, (start, size) in enumerate(spans):
            columns = pl.ds(start, size)
            loads[half, at] = pltpu.make_async_copy(
                weight_ref.at[half, :, columns],
                held_ref.at[half, :, columns],
                in_sems.at[half, at],
            )
            loads[half, at].start()
    lifted = jnp.concatenate([near_ref[...], far_ref[...]], axis=0)
    ordered = dot(one_hot(order_ref[...], lifted.shape[0]), lifted)
    plain = ordered * (1.0 / gain_ref[...].astype(jnp.float32))
    statistics = in_lanes(split_pair(jnp.sum(plain * plain, axis=1, keepdims=True)))
    ordered = ordered.astype(jnp.bfloat16)
    rows = ordered.shape[0] // side
    stores = []
    for at, (start, size) in enumerate(spans):
        loads[1, at].wait()
        ups = dot(ordered, held_ref[1, :, start : start + size])
        for place in range(side):
            second_held[place, :, start : start + size] = ups[
                place * rows : (place + 1) * rows
            ].astype(jnp.bfloat16)
    for place in range(side):
        stores.append(
            pltpu.make_async_copy(
                second_held.at[place], second_refs[place], second_sems.at[place]
            )
        )
        stores[-1].start()
    for at, (start, size) in enumerate(list(spans) + [(hidden, LANES)]):
        if start < hidden:
            loads[0, at].wait()
            gates = dot(ordered, held_ref[0, :, start : start + size])
        else:
            gates = statistics
        for place in range(side):
            first_held[place, :, start : start + size] = blocks_along(gates, side, place).astype(
                jnp.bfloat16
            )
        columns = pl.ds(start, size)
        stores.append(
            pltpu.make_async_copy(
                first_held.at[:, :, columns], first_ref.at[:, :, columns], first_sems.at[at]
            )
        )
        stores[-1].start()
    for store in stores:
        store.wait()


def gate_up(side, order, near, far, gain, weight, tile):
    total, width = order.shape[0], near.shape[1]
    hidden = weight.shape[2]
    rows = total // side
    spans = [(start, min(tile, hidden - start)) for start in range(0, hidden, tile)]
    whole = pl.BlockSpec(memory_space=pltpu.VMEM)
    far_off = pl.BlockSpec(memory_space=pltpu.HBM)
    return pl.pallas_call(
        functools.partial(gate_up_kernel, side, spans),
        out_shape=[jax.ShapeDtypeStruct((side, rows, hidden + LANES), jnp.bfloat16)]
        + [jax.ShapeDtypeStruct((rows, hidden), jnp.bfloat16)] * side,
        in_specs=[whole] * 4 + [far_off],
        out_specs=[far_off] * (1 + side),
        scratch_shapes=[
            pltpu.VMEM(weight.shape, jnp.bfloat16),
            pltpu.VMEM((side, rows, hidden + LANES), jnp.bfloat16),
            pltpu.VMEM((side, rows, hidden), jnp.bfloat16),
            pltpu.SemaphoreType.DMA((2, len(spans))),
            pltpu.SemaphoreType.DMA((len(spans) + 1,)),
            pltpu.SemaphoreType.DMA((side,)),
        ],
        compiler_params=pltpu.CompilerParams(vmem_limit_bytes=48 * MIB),
        cost_estimate=pl.CostEstimate(
            flops=4 * total * width * hidden,
            bytes_accessed=4 * hidden * (width + total),
            transcendentals=0,
        ),
        name="gate_up",
    )(order, near, far, gain.reshape(1, -1), weight)


def spread_dot_kernel(place_ref, rows_ref, weight_ref, kept_ref, sent_ref, total_ref):
    values = dot(rows_ref[...], weight_ref[...])
    blocks = place_ref.shape[0]
    rows = values.shape[0] // blocks
    for at in range(blocks):
        target = pl.ds(pl.multiple_of(place_ref[at], 8), rows)
        total_ref[target, :] = values[at * rows : (at + 1) * rows]
    half = kept_ref.shape[0]
    kept_ref[...] = total_ref[:half]
    sent_ref[...] = total_ref[half:]


def spread_dot(places, values, weight):
    total, width = values.shape[0], weight.shape[1]
    whole = pl.BlockSpec(memory_space=pltpu.VMEM)
    return pl.pallas_call(
        spread_dot_kernel,
        out_shape=[jax.ShapeDtypeStruct((total // 2, width), jnp.float32)] * 2,
        in_specs=[pl.BlockSpec(memory_space=pltpu.SMEM), whole, whole],
        out_specs=[whole] * 2,
        scratch_shapes=[pltpu.VMEM((total, width), jnp.float32)],
        compiler_params=pltpu.CompilerParams(vmem_limit_bytes=20 * MIB),
        cost_estimate=pl.CostEstimate(
            flops=2 * total * weight.size,
            bytes_accessed=2 * weight.size + 2 * total * (weight.shape[0] + 4 * width),
            transcendentals=0,
        ),
        name="spread_dot",
    )(places, values, weight)


def rotary(rows, first_position):
    inverse = np.exp(-math.log(rope_base) * np.arange(HD // 2, dtype=np.float64) * (2.0 / HD))
    angles = (first_position + np.repeat(np.arange(STEPS), rows))[:, None] * inverse[None, :]
    cosine, sine = np.cos(angles), np.sin(angles)
    return np.concatenate([cosine, cosine, -sine, sine], axis=1).astype(np.float32)


def attend_kernel(heads, rows, model, table_ref, cache_ref, *refs):
    out_ref, fresh_ref, kept_ref, query_ref, mix_ref, semaphores = refs
    total = STEPS * rows
    batches, span = kept_ref.shape[2:4]
    edge = (heads + 3) * HD
    stores = []
    for row in range(rows):
        for at in range(2):
            stores.append(
                pltpu.make_async_copy(
                    cache_ref.at[:, pl.ds((2 * (rows + row) + at) * span, span)],
                    kept_ref.at[at, row],
                    semaphores.at[at, row],
                )
            )
            stores[-1].start()
    parts = []
    for start in range(2 * total * span, cache_ref.shape[1], 2 * total):
        pair = cache_ref[0, start : start + 2 * total].astype(jnp.float32)
        for source in range(1, batches):
            pair = pair + cache_ref[source, start : start + 2 * total].astype(jnp.float32)
        parts += [pair[:total], pair[total:]]
    values = jnp.concatenate(parts, axis=1)
    cosine, sine = table_ref[:, :HD], table_ref[:, HD:]
    scale = lax.rsqrt((values[:, edge : edge + 1] + values[:, edge + 1 : edge + 2]) / model + norm_eps)
    parent_scale = lax.rsqrt(
        (values[:, edge + 2 : edge + 3] + values[:, edge + 3 : edge + 4]) / model + norm_eps
    )

    def rotate(block, cosine, sine):
        return block * cosine + pltpu.roll(block, HD // 2, 1) * sine

    def rounded(block):
        return block.astype(jnp.bfloat16).astype(jnp.float32)

    query_ref[...] = jnp.zeros(query_ref.shape, jnp.float32)
    for head in range(heads):
        block = values[:, head * HD : (head + 1) * HD] * scale
        query_ref[:, head, :] = rotate(block, cosine, sine)
    keys = rounded(rotate(values[:, heads * HD : (heads + 1) * HD] * scale, cosine, sine))
    news = rounded(values[:, (heads + 1) * HD : (heads + 2) * HD] * scale)
    parents = values[:, (heads + 2) * HD : edge] * parent_scale
    parent_keys = rounded(rotate(parents[:rows], cosine[:rows], sine[:rows]))
    parent_news = rounded(parents[rows:])
    fresh_ref[0] = jnp.concatenate([keys[:rows], parent_keys], axis=0)
    fresh_ref[1] = keys
    fresh_ref[2] = jnp.concatenate([news[:rows], parent_news], axis=0)
    fresh_ref[3] = news
    queries = query_ref[...].astype(jnp.bfloat16)
    wide = queries.astype(jnp.float32)
    scores = jnp.concatenate(
        [
            lax.dot_general(
                queries[row],
                cache_ref[:, 2 * row * span : (2 * row + 1) * span].reshape(-1, HD),
                (((1,), (1,)), ((), ())),
                preferred_element_type=jnp.float32,
            )
            for row in range(total)
        ],
        axis=0,
    ).reshape(total, queries.shape[1], -1) * (1.0 / math.sqrt(HD))
    extra = [
        jnp.sum(wide * fresh_ref[at][:, None, :], axis=2, keepdims=True) * (1.0 / math.sqrt(HD))
        for at in range(STEPS)
    ]
    later = lax.broadcasted_iota(jnp.int32, extra[1].shape, 0) >= rows
    extra[1] = jnp.where(later, extra[1], -jnp.inf)
    top = jnp.maximum(
        jnp.max(scores, axis=2, keepdims=True), jnp.maximum(extra[0], extra[1])
    )
    weights = jnp.exp(scores - top)
    extra = [jnp.exp(score - top) for score in extra]
    whole = jnp.sum(weights, axis=2, keepdims=True) + extra[0] + extra[1]
    weights = (weights / whole).astype(jnp.bfloat16)
    extra = [rounded(weight / whole) for weight in extra]
    for row in range(total):
        mix_ref[row] = dot(weights[row], cache_ref[:, (2 * row + 1) * span : (2 * row + 2) * span].reshape(-1, HD))
    mix_ref[...] = (
        mix_ref[...]
        + extra[0] * fresh_ref[2][:, None, :]
        + extra[1] * fresh_ref[3][:, None, :]
    )
    for head in range(heads):
        block = mix_ref[:, head, :].astype(jnp.bfloat16)
        for copy in range(out_ref.shape[0]):
            out_ref[copy, :, head * HD : (head + 1) * HD] = block
    for store in stores:
        store.wait()


def attend(returned, heads, rows, past, model):
    batches, total = returned.shape[0], STEPS * rows
    padded = -(-heads // 8) * 8
    whole = pl.BlockSpec(memory_space=pltpu.VMEM)
    return pl.pallas_call(
        functools.partial(attend_kernel, heads, rows, model),
        out_shape=[
            jax.ShapeDtypeStruct((batches, total, heads * HD), jnp.bfloat16),
            jax.ShapeDtypeStruct((2 * STEPS, total, HD), jnp.float32),
            jax.ShapeDtypeStruct((2, rows, batches, past // batches, HD), jnp.bfloat16),
        ],
        grid=(1,),
        in_specs=[whole, pl.BlockSpec(returned.shape, lambda step: (0, 0, 0))],
        out_specs=[whole] * 2 + [pl.BlockSpec(memory_space=pl.ANY)],
        scratch_shapes=[pltpu.VMEM((total, padded, HD), jnp.float32)] * 2
        + [pltpu.SemaphoreType.DMA((2, rows))],
        compiler_params=pltpu.CompilerParams(vmem_limit_bytes=48 * MIB),
        cost_estimate=pl.CostEstimate(
            flops=4 * total * padded * past * HD,
            bytes_accessed=4 * returned.size,
            transcendentals=total * padded * past,
        ),
        name="attend",
    )(jnp.asarray(rotary(rows, past)), returned)


def pick_kernel(index_ref, table_ref, sum_ref, out_ref):
    span = table_ref.shape[1]
    count = index_ref.shape[0] // out_ref.shape[0]

    @pl.loop(0, out_ref.shape[0])
    def _(block):
        for row in range(count):
            out_ref[block, row * span : (row + 1) * span] = table_ref[
                index_ref[block * count + row]
            ]
        out_ref[block, count * span :] = sum_ref[block]


def pick_rows(table, index, sums):
    batches, held, _ = sums.shape
    count = index.shape[0] // batches * table.shape[1]
    whole = pl.BlockSpec(memory_space=pltpu.VMEM)
    return pl.pallas_call(
        pick_kernel,
        out_shape=jax.ShapeDtypeStruct((batches, count + held, LANES), table.dtype),
        in_specs=[pl.BlockSpec(memory_space=pltpu.SMEM), whole, whole],
        out_specs=whole,
        compiler_params=pltpu.CompilerParams(vmem_limit_bytes=32 * MIB),
        cost_estimate=pl.CostEstimate(
            flops=0, bytes_accessed=4 * batches * (count + held) * LANES, transcendentals=0
        ),
        name="pick_rows",
    )(index, table, sums)


def on_device(
    layer_input,
    attn_gain,
    ffn_gain,
    query_weight,
    keyval_weight,
    output_weight,
    gateup_weight,
    down_weight,
    past_cache,
    parent_rows,
):
    batches = lax.axis_size("batch")
    tensors = lax.axis_size("tensor")
    side = math.isqrt(batches)
    chips = tensors // 2
    batch_index = lax.axis_index("batch")
    tensor_index = lax.axis_index("tensor")
    my_major = batch_index // side
    my_chip, my_core = tensor_index // 2, tensor_index % 2
    _, rows, past, kv_width = past_cache.shape
    width = layer_input.shape[2]
    model = width * batches
    head_width = query_weight.shape[1]
    heads = head_width // HD
    hidden = gateup_weight.shape[2]
    both = STEPS * rows
    total = batches * both
    share = total // tensors
    span = past // batches

    with jax.named_scope("cache_spread"):
        pieces = past_cache.reshape(2, rows, batches, span, kv_width).transpose(2, 1, 0, 3, 4)
        spread = exchange(pieces, "batch").reshape(batches * rows, 2 * span, kv_width)

    with jax.named_scope("places"):
        parents = parent_rows.reshape(STEPS, batches, rows)
        origin = jnp.take(parent_rows[0], parent_rows[1], axis=0)
        wanted = jnp.stack([parents[0], origin.reshape(batches, rows)], axis=1).reshape(total)
        place = jnp.arange(total, dtype=jnp.int32)
        inner = place % both
        near = place // both
        input_order = ((inner // rows) * (batches * rows) + near * rows + inner % rows)[:, None]
        row = (my_major + place // (side * both)) % side * side + place // both % side
        row = row * both + inner
        owner = row // share
        lifted_order = (owner % 2 != my_core).astype(jnp.int32) * (total // 2)
        lifted_order = lifted_order + (my_chip - owner // 2 + chips) % chips * share
        lifted_order = (lifted_order + row % share)[:, None]
        block = jnp.arange(batches, dtype=jnp.int32)
        owner = block * both // share
        targets = (owner % 2 != my_core).astype(jnp.int32) * (total // 2)
        targets = targets + (owner // 2 - my_chip + chips) % chips * share
        targets = targets + block * both % share

    with jax.named_scope("project"):
        sums = project_rows(
            batches,
            input_order,
            parent_rows[1][:, None],
            after(layer_input, pieces),
            attn_gain,
            query_weight,
            keyval_weight,
        )

    with jax.named_scope("cache_return"):
        returned = exchange(pick_rows(spread, wanted, sums), "batch")

    with jax.named_scope("attention"):
        attended, fresh, kept = attend(returned, heads, rows, past, model)
        fresh_out = fresh.reshape(2, STEPS, both, kv_width)[:, :, rows:].transpose(0, 2, 1, 3)
        fresh_out = fresh_out.astype(jnp.bfloat16)
        cache_out = kept.reshape(2, rows, past, kv_width)
        attended = exchange(attended, "batch").reshape(total, head_width)

    with jax.named_scope("output_projection"):
        own_inputs = lax.dynamic_slice_in_dim(
            layer_input, tensor_index * (share // STEPS), share // STEPS, 1
        )
        own_inputs = (
            own_inputs.reshape(STEPS, share // both, rows, width)
            .transpose(1, 0, 2, 3)
            .reshape(share, width)
        )
        mixed = add_over_tensor(*spread_dot(targets, attended, output_weight))
        residual = own_inputs.astype(jnp.float32) + mixed
        lifted = (residual * ffn_gain.astype(jnp.float32)).astype(jnp.bfloat16)
        near = jnp.concatenate(
            [lifted] + [shift_chips(lifted, count) for count in range(1, chips)], axis=0
        )
        far = swap_cores(near)

    with jax.named_scope("gate_up"):
        blocks = gate_up(side, lifted_order, near, far, ffn_gain, gateup_weight, 768)
        gates, ups = add_crossed(blocks[0], blocks[1:])
        mean = (gates[:, hidden] + gates[:, hidden + 1]) / model
        scale = lax.rsqrt(mean + norm_eps)[:, None]
        gates, ups = gates[:, :hidden] * scale, ups * scale
        activated = (jax.nn.silu(gates) * ups).astype(jnp.bfloat16)
        activated = gather_all(activated, "batch")

    with jax.named_scope("down_projection"):
        lowered = add_over_tensor(*spread_dot(targets, activated, down_weight))
        final = (residual + lowered).astype(jnp.bfloat16)
        layer_out = (
            final.reshape(share // both, STEPS, rows, width)
            .transpose(1, 0, 2, 3)
            .reshape(STEPS, share // STEPS, width)
        )
    return layer_out, cache_out, fresh_out


def solution(mesh):
    return jax.shard_map(
        on_device,
        mesh=mesh,
        in_specs=(
            P(None, None, "batch"),
            P("batch"),
            P("batch"),
            P("batch", "tensor"),
            P(None, "batch", "tensor"),
            P("tensor", "batch"),
            P(None, "batch", "tensor"),
            P("tensor", "batch"),
            P(None, "batch", None, "tensor"),
            P(),
        ),
        out_specs=(
            P(None, "tensor", "batch"),
            P(None, "batch", None, "tensor"),
            P(None, "batch", None, "tensor"),
        ),
        check_vma=False,
    )
```

```python
import functools
import math

import jax
import jax.numpy as jnp
import numpy as np
from jax import lax
from jax.experimental import pallas as pl
from jax.experimental.pallas import tpu as pltpu
from jax.sharding import PartitionSpec as P

HD = 128
LANES = 128
STEPS = 2
MIB = 1024 * 1024

rope_base = 1000000.0
norm_eps = 1e-05


def exchange(blocks, axis):
    return lax.all_to_all(blocks, axis, split_axis=0, concat_axis=0, tiled=True)


def gather_all(block, axis):
    copies = jnp.broadcast_to(block[None], (lax.axis_size(axis),) + block.shape)
    gathered = exchange(lax.optimization_barrier(copies), axis)
    return gathered.reshape((-1,) + block.shape[1:])


def after(value, earlier):
    return lax.optimization_barrier((value, earlier))[0]


def shift_along(block, minor_axis, count):
    side = math.isqrt(lax.axis_size("batch"))
    pairs = []
    for major in range(side):
        for minor in range(side):
            target = (
                (major, (minor + count) % side) if minor_axis else ((major + count) % side, minor)
            )
            pairs.append((major * side + minor, target[0] * side + target[1]))
    return lax.ppermute(block, "batch", pairs)


def shift_chips(block, count):
    size = lax.axis_size("tensor")
    return lax.ppermute(block, "tensor", [(at, (at + 2 * count) % size) for at in range(size)])


def swap_cores(block):
    size = lax.axis_size("tensor")
    return lax.ppermute(block, "tensor", [(at, at ^ 1) for at in range(size)])


def fold_kernel(count, *refs):
    sources, targets = refs[:count], refs[count:]
    terms = []
    for source in sources:
        terms += [source] if len(source.shape) == 2 else [source.at[at] for at in range(source.shape[0])]
    total = terms[0][...].astype(jnp.float32)
    for term in terms[1:]:
        total = total + term[...].astype(jnp.float32)
    rows = total.shape[0] // len(targets)
    for place, target in enumerate(targets):
        target[...] = total[place * rows : (place + 1) * rows].astype(target.dtype)


def fold(sources, pieces):
    rows, columns = sources[0].shape[-2:]
    kinds = [jnp.float32] + [jnp.bfloat16] * (pieces - 1)
    whole = pl.BlockSpec(memory_space=pltpu.VMEM)
    return pl.pallas_call(
        functools.partial(fold_kernel, len(sources)),
        out_shape=[jax.ShapeDtypeStruct((rows // pieces, columns), kind) for kind in kinds],
        in_specs=[whole] * len(sources),
        out_specs=[whole] * pieces,
        compiler_params=pltpu.CompilerParams(vmem_limit_bytes=32 * MIB),
        cost_estimate=pl.CostEstimate(flops=1, bytes_accessed=1, transcendentals=0),
        name="fold",
    )(*sources)


def exchange_minor(blocks):
    side = math.isqrt(lax.axis_size("batch"))
    groups = [[major * side + minor for minor in range(side)] for major in range(side)]
    return lax.all_to_all(
        blocks, "batch", split_axis=0, concat_axis=0, tiled=True, axis_index_groups=groups
    )


def add_along(own, terms):
    return functools.reduce(lambda total, term: total + term.astype(jnp.float32), terms, own)


def add_crossed(first, second):
    side = len(second)
    others = range(1, side)
    moved = [second[0]] + [shift_along(second[count], 0, count) for count in others]
    arrived = exchange_minor(first)
    summed = fold([arrived], side)
    first = add_along(summed[0], [shift_along(summed[count], 0, count) for count in others])
    crossed = add_along(moved[0].astype(jnp.float32), moved[1:]).astype(jnp.bfloat16)
    crossed = exchange_minor(crossed.reshape((side, -1) + crossed.shape[1:]))
    return first, jnp.sum(crossed.astype(jnp.float32), axis=0)


def add_over_tensor(kept, sent):
    chips = lax.axis_size("tensor") // 2
    pieces = fold([kept, swap_cores(sent)], chips)
    total = pieces[0]
    for count in range(1, chips):
        total = total + shift_chips(pieces[count], count).astype(jnp.float32)
    return total


def blocks_along(values, side, place):
    rows = values.shape[0] // (side * side)
    return jnp.concatenate(
        [
            values[(major * side + place) * rows : (major * side + place + 1) * rows]
            for major in range(side)
        ],
        axis=0,
    )


def one_hot(index, count):
    places = lax.broadcasted_iota(jnp.int32, (index.shape[0], count), 1)
    return jnp.where(places == index, 1.0, 0.0).astype(jnp.bfloat16)


def dot(left, right):
    return jnp.dot(left, right, preferred_element_type=jnp.float32)


def split_pair(values):
    high = values.astype(jnp.bfloat16).astype(jnp.float32)
    return [high, values - high]


def in_lanes(columns):
    lanes = lax.broadcasted_iota(jnp.int32, (columns[0].shape[0], LANES), 1)
    packed = jnp.zeros(lanes.shape, jnp.float32)
    for place, value in enumerate(columns):
        packed = jnp.where(lanes == place, value, packed)
    return packed


def project_kernel(
    order_ref, parent_ref, input_ref, gain_ref, query_ref, keyval_ref, out_ref
):
    steps, count, width = input_ref.shape
    source = input_ref[...].reshape(steps * count, width)
    gain = gain_ref[...].astype(jnp.float32)
    order = order_ref[...]
    is_key = order < count
    own = dot(one_hot(order, steps * count), source)
    parents = dot(one_hot(parent_ref[...], count), input_ref[0]).astype(jnp.bfloat16)
    parents = dot(one_hot(jnp.where(is_key, order, order - count), count), parents)
    statistics = split_pair(jnp.sum(own * own, axis=1, keepdims=True)) + split_pair(
        jnp.sum(parents * parents, axis=1, keepdims=True)
    )
    own = (own * gain).astype(jnp.bfloat16)
    parents = (parents * gain).astype(jnp.bfloat16)
    values = jnp.concatenate(
        [
            dot(own, query_ref[...]),
            dot(own, keyval_ref[0]),
            dot(own, keyval_ref[1]),
            jnp.where(is_key, dot(parents, keyval_ref[0]), dot(parents, keyval_ref[1])),
            in_lanes(statistics),
        ],
        axis=1,
    ).astype(jnp.float32)
    blocks, held, _ = out_ref.shape
    rows = values.shape[0] // blocks
    for block in range(blocks):
        part = values[block * rows : (block + 1) * rows]
        for at in range(held // (2 * rows)):
            pair = [
                part[:, (2 * at + side) * LANES : (2 * at + side + 1) * LANES] for side in range(2)
            ]
            out_ref[block, 2 * at * rows : 2 * (at + 1) * rows] = jnp.concatenate(
                pair, axis=0
            ).astype(jnp.bfloat16)


def project_rows(batches, order, parents, layer_input, gain, query_weight, keyval_weight):
    total = order.shape[0]
    columns = query_weight.shape[1] + 3 * keyval_weight.shape[2] + LANES
    held = total // batches * columns // LANES
    whole = pl.BlockSpec(memory_space=pltpu.VMEM)
    return pl.pallas_call(
        project_kernel,
        out_shape=jax.ShapeDtypeStruct((batches, held, LANES), jnp.bfloat16),
        in_specs=[whole] * 6,
        out_specs=whole,
        compiler_params=pltpu.CompilerParams(vmem_limit_bytes=48 * MIB),
        cost_estimate=pl.CostEstimate(
            flops=2 * total * columns * gain.shape[0],
            bytes_accessed=2 * (gain.shape[0] + total) * columns,
            transcendentals=0,
        ),
        name="project_rows",
    )(order, parents, layer_input, gain.reshape(1, -1), query_weight, keyval_weight)


def gate_up_kernel(side, spans, order_ref, near_ref, far_ref, gain_ref, weight_ref, *refs):
    first_ref, second_refs = refs[0], refs[1 : 1 + side]
    held_ref, first_held, second_held, in_sems, first_sems, second_sems = refs[1 + side :]
    hidden = weight_ref.shape[2]
    loads = {}
    for half in (1, 0):
        for at, (start, size) in enumerate(spans):
            columns = pl.ds(start, size)
            loads[half, at] = pltpu.make_async_copy(
                weight_ref.at[half, :, columns],
                held_ref.at[half, :, columns],
                in_sems.at[half, at],
            )
    order = [(half, at) for half in (1, 0) for at in range(len(spans))]
    ahead = 4
    for key in order[:ahead]:
        loads[key].start()

    def arrived(half, at):
        step = order.index((half, at))
        if step + ahead < len(order):
            loads[order[step + ahead]].start()
        loads[half, at].wait()

    lifted = jnp.concatenate([near_ref[...], far_ref[...]], axis=0)
    ordered = dot(one_hot(order_ref[...], lifted.shape[0]), lifted)
    plain = ordered * (1.0 / gain_ref[...].astype(jnp.float32))
    statistics = in_lanes(split_pair(jnp.sum(plain * plain, axis=1, keepdims=True)))
    ordered = ordered.astype(jnp.bfloat16)
    rows = ordered.shape[0] // side
    stores = []
    for at, (start, size) in enumerate(spans):
        arrived(1, at)
        ups = dot(ordered, held_ref[1, :, start : start + size])
        for place in range(side):
            second_held[place, :, start : start + size] = ups[
                place * rows : (place + 1) * rows
            ].astype(jnp.bfloat16)
    for place in range(side):
        stores.append(
            pltpu.make_async_copy(
                second_held.at[place], second_refs[place], second_sems.at[place]
            )
        )
        stores[-1].start()
    for at, (start, size) in enumerate(list(spans) + [(hidden, LANES)]):
        if start < hidden:
            arrived(0, at)
            gates = dot(ordered, held_ref[0, :, start : start + size])
        else:
            gates = statistics
        for place in range(side):
            first_held[place, :, start : start + size] = blocks_along(gates, side, place).astype(
                jnp.bfloat16
            )
        columns = pl.ds(start, size)
        stores.append(
            pltpu.make_async_copy(
                first_held.at[:, :, columns], first_ref.at[:, :, columns], first_sems.at[at]
            )
        )
        stores[-1].start()
    for store in stores:
        store.wait()


def gate_up(side, order, near, far, gain, weight, tile):
    total, width = order.shape[0], near.shape[1]
    hidden = weight.shape[2]
    rows = total // side
    edges = [0] + list(range(hidden % tile or tile, hidden + 1, tile))
    spans = [(start, stop - start) for start, stop in zip(edges, edges[1:])]
    whole = pl.BlockSpec(memory_space=pltpu.VMEM)
    far_off = pl.BlockSpec(memory_space=pltpu.HBM)
    return pl.pallas_call(
        functools.partial(gate_up_kernel, side, spans),
        out_shape=[jax.ShapeDtypeStruct((side, rows, hidden + LANES), jnp.bfloat16)]
        + [jax.ShapeDtypeStruct((rows, hidden), jnp.bfloat16)] * side,
        in_specs=[whole] * 4 + [far_off],
        out_specs=[far_off] * (1 + side),
        scratch_shapes=[
            pltpu.VMEM(weight.shape, jnp.bfloat16),
            pltpu.VMEM((side, rows, hidden + LANES), jnp.bfloat16),
            pltpu.VMEM((side, rows, hidden), jnp.bfloat16),
            pltpu.SemaphoreType.DMA((2, len(spans))),
            pltpu.SemaphoreType.DMA((len(spans) + 1,)),
            pltpu.SemaphoreType.DMA((side,)),
        ],
        compiler_params=pltpu.CompilerParams(vmem_limit_bytes=58 * MIB),
        cost_estimate=pl.CostEstimate(
            flops=4 * total * width * hidden,
            bytes_accessed=4 * hidden * (width + total),
            transcendentals=0,
        ),
        name="gate_up",
    )(order, near, far, gain.reshape(1, -1), weight)


def spread_dot_kernel(place_ref, rows_ref, weight_ref, kept_ref, sent_ref, total_ref):
    values = dot(rows_ref[...], weight_ref[...])
    blocks = place_ref.shape[0]
    rows = values.shape[0] // blocks
    for at in range(blocks):
        target = pl.ds(pl.multiple_of(place_ref[at], 8), rows)
        total_ref[target, :] = values[at * rows : (at + 1) * rows]
    half = kept_ref.shape[0]
    kept_ref[...] = total_ref[:half]
    sent_ref[...] = total_ref[half:]


def spread_dot(places, values, weight):
    total, width = values.shape[0], weight.shape[1]
    whole = pl.BlockSpec(memory_space=pltpu.VMEM)
    return pl.pallas_call(
        spread_dot_kernel,
        out_shape=[jax.ShapeDtypeStruct((total // 2, width), jnp.float32)] * 2,
        in_specs=[pl.BlockSpec(memory_space=pltpu.SMEM), whole, whole],
        out_specs=[whole] * 2,
        scratch_shapes=[pltpu.VMEM((total, width), jnp.float32)],
        compiler_params=pltpu.CompilerParams(vmem_limit_bytes=20 * MIB),
        cost_estimate=pl.CostEstimate(
            flops=2 * total * weight.size,
            bytes_accessed=2 * weight.size + 2 * total * (weight.shape[0] + 4 * width),
            transcendentals=0,
        ),
        name="spread_dot",
    )(places, values, weight)


def rotary(rows, first_position):
    inverse = np.exp(-math.log(rope_base) * np.arange(HD // 2, dtype=np.float64) * (2.0 / HD))
    angles = (first_position + np.repeat(np.arange(STEPS), rows))[:, None] * inverse[None, :]
    cosine, sine = np.cos(angles), np.sin(angles)
    return np.concatenate([cosine, cosine, -sine, sine], axis=1).astype(np.float32)


def attend_kernel(heads, rows, model, table_ref, cache_ref, *refs):
    out_ref, fresh_ref, kept_ref, query_ref, mix_ref, semaphores = refs
    total = STEPS * rows
    batches, span = kept_ref.shape[2:4]
    edge = (heads + 3) * HD
    stores = []
    for row in range(rows):
        for at in range(2):
            stores.append(
                pltpu.make_async_copy(
                    cache_ref.at[:, pl.ds((2 * (rows + row) + at) * span, span)],
                    kept_ref.at[at, row],
                    semaphores.at[at, row],
                )
            )
            stores[-1].start()
    parts = []
    for start in range(2 * total * span, cache_ref.shape[1], 2 * total):
        pair = cache_ref[0, start : start + 2 * total].astype(jnp.float32)
        for source in range(1, batches):
            pair = pair + cache_ref[source, start : start + 2 * total].astype(jnp.float32)
        parts += [pair[:total], pair[total:]]
    values = jnp.concatenate(parts, axis=1)
    cosine, sine = table_ref[:, :HD], table_ref[:, HD:]
    scale = lax.rsqrt((values[:, edge : edge + 1] + values[:, edge + 1 : edge + 2]) / model + norm_eps)
    parent_scale = lax.rsqrt(
        (values[:, edge + 2 : edge + 3] + values[:, edge + 3 : edge + 4]) / model + norm_eps
    )

    def rotate(block, cosine, sine):
        return block * cosine + pltpu.roll(block, HD // 2, 1) * sine

    def rounded(block):
        return block.astype(jnp.bfloat16).astype(jnp.float32)

    query_ref[...] = jnp.zeros(query_ref.shape, jnp.float32)
    for head in range(heads):
        block = values[:, head * HD : (head + 1) * HD] * scale
        query_ref[:, head, :] = rotate(block, cosine, sine)
    keys = rounded(rotate(values[:, heads * HD : (heads + 1) * HD] * scale, cosine, sine))
    news = rounded(values[:, (heads + 1) * HD : (heads + 2) * HD] * scale)
    parents = values[:, (heads + 2) * HD : edge] * parent_scale
    parent_keys = rounded(rotate(parents[:rows], cosine[:rows], sine[:rows]))
    parent_news = rounded(parents[rows:])
    fresh_ref[0] = jnp.concatenate([keys[:rows], parent_keys], axis=0)
    fresh_ref[1] = keys
    fresh_ref[2] = jnp.concatenate([news[:rows], parent_news], axis=0)
    fresh_ref[3] = news
    queries = query_ref[...].astype(jnp.bfloat16)
    wide = queries.astype(jnp.float32)
    scores = jnp.concatenate(
        [
            lax.dot_general(
                queries[row],
                cache_ref[:, 2 * row * span : (2 * row + 1) * span].reshape(-1, HD),
                (((1,), (1,)), ((), ())),
                preferred_element_type=jnp.float32,
            )
            for row in range(total)
        ],
        axis=0,
    ).reshape(total, queries.shape[1], -1) * (1.0 / math.sqrt(HD))
    extra = [
        jnp.sum(wide * fresh_ref[at][:, None, :], axis=2, keepdims=True) * (1.0 / math.sqrt(HD))
        for at in range(STEPS)
    ]
    later = lax.broadcasted_iota(jnp.int32, extra[1].shape, 0) >= rows
    extra[1] = jnp.where(later, extra[1], -jnp.inf)
    top = jnp.maximum(
        jnp.max(scores, axis=2, keepdims=True), jnp.maximum(extra[0], extra[1])
    )
    weights = jnp.exp(scores - top)
    extra = [jnp.exp(score - top) for score in extra]
    whole = jnp.sum(weights, axis=2, keepdims=True) + extra[0] + extra[1]
    weights = (weights / whole).astype(jnp.bfloat16)
    extra = [rounded(weight / whole) for weight in extra]
    for row in range(total):
        mix_ref[row] = dot(weights[row], cache_ref[:, (2 * row + 1) * span : (2 * row + 2) * span].reshape(-1, HD))
    mix_ref[...] = (
        mix_ref[...]
        + extra[0] * fresh_ref[2][:, None, :]
        + extra[1] * fresh_ref[3][:, None, :]
    )
    for head in range(heads):
        block = mix_ref[:, head, :].astype(jnp.bfloat16)
        for copy in range(out_ref.shape[0]):
            out_ref[copy, :, head * HD : (head + 1) * HD] = block
    for store in stores:
        store.wait()


def attend(returned, heads, rows, past, model):
    batches, total = returned.shape[0], STEPS * rows
    padded = -(-heads // 8) * 8
    whole = pl.BlockSpec(memory_space=pltpu.VMEM)
    return pl.pallas_call(
        functools.partial(attend_kernel, heads, rows, model),
        out_shape=[
            jax.ShapeDtypeStruct((batches, total, heads * HD), jnp.bfloat16),
            jax.ShapeDtypeStruct((2 * STEPS, total, HD), jnp.float32),
            jax.ShapeDtypeStruct((2, rows, batches, past // batches, HD), jnp.bfloat16),
        ],
        grid=(1,),
        in_specs=[whole, pl.BlockSpec(returned.shape, lambda step: (0, 0, 0))],
        out_specs=[whole] * 2 + [pl.BlockSpec(memory_space=pl.ANY)],
        scratch_shapes=[pltpu.VMEM((total, padded, HD), jnp.float32)] * 2
        + [pltpu.SemaphoreType.DMA((2, rows))],
        compiler_params=pltpu.CompilerParams(vmem_limit_bytes=48 * MIB),
        cost_estimate=pl.CostEstimate(
            flops=4 * total * padded * past * HD,
            bytes_accessed=4 * returned.size,
            transcendentals=total * padded * past,
        ),
        name="attend",
    )(jnp.asarray(rotary(rows, past)), returned)


def pick_kernel(index_ref, table_ref, sum_ref, out_ref):
    span = table_ref.shape[1]
    count = index_ref.shape[0] // out_ref.shape[0]

    @pl.loop(0, out_ref.shape[0])
    def _(block):
        for row in range(count):
            out_ref[block, row * span : (row + 1) * span] = table_ref[
                index_ref[block * count + row]
            ]
        out_ref[block, count * span :] = sum_ref[block]


def pick_rows(table, index, sums):
    batches, held, _ = sums.shape
    count = index.shape[0] // batches * table.shape[1]
    whole = pl.BlockSpec(memory_space=pltpu.VMEM)
    return pl.pallas_call(
        pick_kernel,
        out_shape=jax.ShapeDtypeStruct((batches, count + held, LANES), table.dtype),
        in_specs=[pl.BlockSpec(memory_space=pltpu.SMEM), whole, whole],
        out_specs=whole,
        compiler_params=pltpu.CompilerParams(vmem_limit_bytes=32 * MIB),
        cost_estimate=pl.CostEstimate(
            flops=0, bytes_accessed=4 * batches * (count + held) * LANES, transcendentals=0
        ),
        name="pick_rows",
    )(index, table, sums)


def on_device(
    layer_input,
    attn_gain,
    ffn_gain,
    query_weight,
    keyval_weight,
    output_weight,
    gateup_weight,
    down_weight,
    past_cache,
    parent_rows,
):
    batches = lax.axis_size("batch")
    tensors = lax.axis_size("tensor")
    side = math.isqrt(batches)
    chips = tensors // 2
    batch_index = lax.axis_index("batch")
    tensor_index = lax.axis_index("tensor")
    my_major = batch_index // side
    my_chip, my_core = tensor_index // 2, tensor_index % 2
    _, rows, past, kv_width = past_cache.shape
    width = layer_input.shape[2]
    model = width * batches
    head_width = query_weight.shape[1]
    heads = head_width // HD
    hidden = gateup_weight.shape[2]
    both = STEPS * rows
    total = batches * both
    share = total // tensors
    span = past // batches

    with jax.named_scope("cache_spread"):
        pieces = past_cache.reshape(2, rows, batches, span, kv_width).transpose(2, 1, 0, 3, 4)
        spread = exchange(pieces, "batch").reshape(batches * rows, 2 * span, kv_width)

    with jax.named_scope("places"):
        parents = parent_rows.reshape(STEPS, batches, rows)
        origin = jnp.take(parent_rows[0], parent_rows[1], axis=0)
        wanted = jnp.stack([parents[0], origin.reshape(batches, rows)], axis=1).reshape(total)
        place = jnp.arange(total, dtype=jnp.int32)
        inner = place % both
        near = place // both
        input_order = ((inner // rows) * (batches * rows) + near * rows + inner % rows)[:, None]
        row = (my_major + place // (side * both)) % side * side + place // both % side
        row = row * both + inner
        owner = row // share
        lifted_order = (owner % 2 != my_core).astype(jnp.int32) * (total // 2)
        lifted_order = lifted_order + (my_chip - owner // 2 + chips) % chips * share
        lifted_order = (lifted_order + row % share)[:, None]
        block = jnp.arange(batches, dtype=jnp.int32)
        owner = block * both // share
        targets = (owner % 2 != my_core).astype(jnp.int32) * (total // 2)
        targets = targets + (owner // 2 - my_chip + chips) % chips * share
        targets = targets + block * both % share

    with jax.named_scope("project"):
        sums = project_rows(
            batches,
            input_order,
            parent_rows[1][:, None],
            after(layer_input, pieces),
            attn_gain,
            query_weight,
            keyval_weight,
        )

    with jax.named_scope("cache_return"):
        ready = after(wanted, (lifted_order, targets))
        returned = exchange(pick_rows(spread, ready, sums), "batch")

    with jax.named_scope("attention"):
        attended, fresh, kept = attend(returned, heads, rows, past, model)
        fresh_out = fresh.reshape(2, STEPS, both, kv_width)[:, :, rows:].transpose(0, 2, 1, 3)
        fresh_out = fresh_out.astype(jnp.bfloat16)
        cache_out = kept.reshape(2, rows, past, kv_width)
        attended = exchange(attended, "batch").reshape(total, head_width)

    with jax.named_scope("output_projection"):
        own_inputs = lax.dynamic_slice_in_dim(
            layer_input, tensor_index * (share // STEPS), share // STEPS, 1
        )
        own_inputs = (
            own_inputs.reshape(STEPS, share // both, rows, width)
            .transpose(1, 0, 2, 3)
            .reshape(share, width)
        )
        mixed = add_over_tensor(*spread_dot(targets, attended, output_weight))
        residual = own_inputs.astype(jnp.float32) + mixed
        lifted = (residual * ffn_gain.astype(jnp.float32)).astype(jnp.bfloat16)
        near = jnp.concatenate(
            [lifted] + [shift_chips(lifted, count) for count in range(1, chips)], axis=0
        )
        far = swap_cores(near)

    with jax.named_scope("gate_up"):
        blocks = gate_up(side, lifted_order, near, far, ffn_gain, gateup_weight, 768)
        gates, ups = add_crossed(blocks[0], blocks[1:])
        mean = (gates[:, hidden] + gates[:, hidden + 1]) / model
        scale = lax.rsqrt(mean + norm_eps)[:, None]
        gates, ups = gates[:, :hidden] * scale, ups * scale
        activated = (jax.nn.silu(gates) * ups).astype(jnp.bfloat16)
        activated = gather_all(activated, "batch")

    with jax.named_scope("down_projection"):
        lowered = add_over_tensor(*spread_dot(targets, activated, down_weight))
        final = (residual + lowered).astype(jnp.bfloat16)
        layer_out = (
            final.reshape(share // both, STEPS, rows, width)
            .transpose(1, 0, 2, 3)
            .reshape(STEPS, share // STEPS, width)
        )
    return layer_out, cache_out, fresh_out


def solution(mesh):
    return jax.shard_map(
        on_device,
        mesh=mesh,
        in_specs=(
            P(None, None, "batch"),
            P("batch"),
            P("batch"),
            P("batch", "tensor"),
            P(None, "batch", "tensor"),
            P("tensor", "batch"),
            P(None, "batch", "tensor"),
            P("tensor", "batch"),
            P(None, "batch", None, "tensor"),
            P(),
        ),
        out_specs=(
            P(None, "tensor", "batch"),
            P(None, "batch", None, "tensor"),
            P(None, "batch", None, "tensor"),
        ),
        check_vma=False,
    )
```

```python
import functools
import math

import jax
import jax.numpy as jnp
import numpy as np
from jax import lax
from jax.experimental import pallas as pl
from jax.experimental.pallas import tpu as pltpu
from jax.sharding import PartitionSpec as P

HD = 128
LANES = 128
STEPS = 2
MIB = 1024 * 1024

rope_base = 1000000.0
norm_eps = 1e-05


def exchange(blocks, axis):
    return lax.all_to_all(blocks, axis, split_axis=0, concat_axis=0, tiled=True)


def after(value, earlier):
    return lax.optimization_barrier((value, earlier))[0]


def shift_along(block, minor_axis, count):
    side = math.isqrt(lax.axis_size("batch"))
    pairs = []
    for major in range(side):
        for minor in range(side):
            target = (
                (major, (minor + count) % side) if minor_axis else ((major + count) % side, minor)
            )
            pairs.append((major * side + minor, target[0] * side + target[1]))
    return lax.ppermute(block, "batch", pairs)


def shift_chips(block, count):
    size = lax.axis_size("tensor")
    return lax.ppermute(block, "tensor", [(at, (at + 2 * count) % size) for at in range(size)])


def swap_cores(block):
    size = lax.axis_size("tensor")
    return lax.ppermute(block, "tensor", [(at, at ^ 1) for at in range(size)])


def fold_kernel(count, *refs):
    sources, targets = refs[:count], refs[count:]
    terms = []
    for source in sources:
        terms += [source] if len(source.shape) == 2 else [source.at[at] for at in range(source.shape[0])]
    total = terms[0][...].astype(jnp.float32)
    for term in terms[1:]:
        total = total + term[...].astype(jnp.float32)
    rows = total.shape[0] // len(targets)
    for place, target in enumerate(targets):
        target[...] = total[place * rows : (place + 1) * rows].astype(target.dtype)


def fold(sources, pieces):
    rows, columns = sources[0].shape[-2:]
    kinds = [jnp.float32] + [jnp.bfloat16] * (pieces - 1)
    whole = pl.BlockSpec(memory_space=pltpu.VMEM)
    return pl.pallas_call(
        functools.partial(fold_kernel, len(sources)),
        out_shape=[jax.ShapeDtypeStruct((rows // pieces, columns), kind) for kind in kinds],
        in_specs=[whole] * len(sources),
        out_specs=[whole] * pieces,
        compiler_params=pltpu.CompilerParams(vmem_limit_bytes=32 * MIB),
        cost_estimate=pl.CostEstimate(flops=1, bytes_accessed=1, transcendentals=0),
        name="fold",
    )(*sources)


def exchange_minor(blocks):
    side = math.isqrt(lax.axis_size("batch"))
    groups = [[major * side + minor for minor in range(side)] for major in range(side)]
    return lax.all_to_all(
        blocks, "batch", split_axis=0, concat_axis=0, tiled=True, axis_index_groups=groups
    )


def exchange_minor(blocks):
    side = math.isqrt(lax.axis_size("batch"))
    groups = [[major * side + minor for minor in range(side)] for major in range(side)]
    return lax.all_to_all(
        blocks, "batch", split_axis=0, concat_axis=0, tiled=True, axis_index_groups=groups
    )


def add_along(own, terms):
    return functools.reduce(lambda total, term: total + term.astype(jnp.float32), terms, own)


def stack_kernel(*refs):
    sources, target = refs[:-1], refs[-1]
    total = sources[0][...].astype(jnp.float32)
    for source in sources[1:]:
        total = total + source[...].astype(jnp.float32)
    rows = target.shape[1]
    for place in range(target.shape[0]):
        target[place] = total[place * rows : (place + 1) * rows].astype(target.dtype)


def fold_stacked(sources):
    rows, columns = sources[0].shape
    shape = (len(sources), rows // len(sources), columns)
    whole = pl.BlockSpec(memory_space=pltpu.VMEM)
    return pl.pallas_call(
        stack_kernel,
        out_shape=jax.ShapeDtypeStruct(shape, jnp.bfloat16),
        in_specs=[whole] * len(sources),
        out_specs=whole,
        compiler_params=pltpu.CompilerParams(vmem_limit_bytes=32 * MIB),
        cost_estimate=pl.CostEstimate(flops=1, bytes_accessed=1, transcendentals=0),
        name="fold_stacked",
    )(*sources)


def activate_kernel(model, own_ref, *refs):
    terms, crossed_ref, out_ref = refs[:-2], refs[-2], refs[-1]
    hidden = out_ref.shape[2]
    gates = own_ref[...]
    for term in terms:
        gates = gates + term[...].astype(jnp.float32)
    ups = crossed_ref[0].astype(jnp.float32)
    for place in range(1, crossed_ref.shape[0]):
        ups = ups + crossed_ref[place].astype(jnp.float32)
    mean = (gates[:, hidden : hidden + 1] + gates[:, hidden + 1 : hidden + 2]) / model
    scale = lax.rsqrt(mean + norm_eps)
    gates, ups = gates[:, :hidden] * scale, ups * scale
    activated = (gates / (1.0 + jnp.exp(-gates)) * ups).astype(jnp.bfloat16)
    for copy in range(out_ref.shape[0]):
        out_ref[copy] = activated


def activate(own, terms, crossed, model, copies):
    _, rows, hidden = crossed.shape
    whole = pl.BlockSpec(memory_space=pltpu.VMEM)
    return pl.pallas_call(
        functools.partial(activate_kernel, model),
        out_shape=jax.ShapeDtypeStruct((copies, rows, hidden), jnp.bfloat16),
        in_specs=[whole] * (2 + len(terms)),
        out_specs=whole,
        compiler_params=pltpu.CompilerParams(vmem_limit_bytes=32 * MIB),
        cost_estimate=pl.CostEstimate(
            flops=8 * rows * hidden,
            bytes_accessed=2 * copies * rows * hidden,
            transcendentals=rows * hidden,
        ),
        name="activate",
    )(own, *terms, crossed)


def add_crossed(first, second):
    side = len(second)
    others = range(1, side)
    moved = [second[0]] + [shift_along(second[count], 0, count) for count in others]
    summed = fold([exchange_minor(first)], side)
    terms = [shift_along(summed[count], 0, count) for count in others]
    return summed[0], terms, exchange_minor(fold_stacked(moved))


def add_over_tensor(kept, sent):
    chips = lax.axis_size("tensor") // 2
    pieces = fold([kept, swap_cores(sent)], chips)
    total = pieces[0]
    for count in range(1, chips):
        total = total + shift_chips(pieces[count], count).astype(jnp.float32)
    return total


def blocks_along(values, side, place):
    rows = values.shape[0] // (side * side)
    return jnp.concatenate(
        [
            values[(major * side + place) * rows : (major * side + place + 1) * rows]
            for major in range(side)
        ],
        axis=0,
    )


def one_hot(index, count):
    places = lax.broadcasted_iota(jnp.int32, (index.shape[0], count), 1)
    return jnp.where(places == index, 1.0, 0.0).astype(jnp.bfloat16)


def dot(left, right):
    return jnp.dot(left, right, preferred_element_type=jnp.float32)


def split_pair(values):
    high = values.astype(jnp.bfloat16).astype(jnp.float32)
    return [high, values - high]


def in_lanes(columns):
    lanes = lax.broadcasted_iota(jnp.int32, (columns[0].shape[0], LANES), 1)
    packed = jnp.zeros(lanes.shape, jnp.float32)
    for place, value in enumerate(columns):
        packed = jnp.where(lanes == place, value, packed)
    return packed


def project_kernel(
    order_ref, parent_ref, input_ref, gain_ref, query_ref, keyval_ref, out_ref
):
    steps, count, width = input_ref.shape
    source = input_ref[...].reshape(steps * count, width)
    gain = gain_ref[...].astype(jnp.float32)
    order = order_ref[...]
    is_key = order < count
    own = dot(one_hot(order, steps * count), source)
    parents = dot(one_hot(parent_ref[...], count), input_ref[0]).astype(jnp.bfloat16)
    parents = dot(one_hot(jnp.where(is_key, order, order - count), count), parents)
    statistics = split_pair(jnp.sum(own * own, axis=1, keepdims=True)) + split_pair(
        jnp.sum(parents * parents, axis=1, keepdims=True)
    )
    own = (own * gain).astype(jnp.bfloat16)
    parents = (parents * gain).astype(jnp.bfloat16)
    values = jnp.concatenate(
        [
            dot(own, query_ref[...]),
            dot(own, keyval_ref[0]),
            dot(own, keyval_ref[1]),
            jnp.where(is_key, dot(parents, keyval_ref[0]), dot(parents, keyval_ref[1])),
            in_lanes(statistics),
        ],
        axis=1,
    ).astype(jnp.float32)
    blocks, held, _ = out_ref.shape
    rows = values.shape[0] // blocks
    for block in range(blocks):
        part = values[block * rows : (block + 1) * rows]
        for at in range(held // (2 * rows)):
            pair = [
                part[:, (2 * at + side) * LANES : (2 * at + side + 1) * LANES] for side in range(2)
            ]
            out_ref[block, 2 * at * rows : 2 * (at + 1) * rows] = jnp.concatenate(
                pair, axis=0
            ).astype(jnp.bfloat16)


def project_rows(batches, order, parents, layer_input, gain, query_weight, keyval_weight):
    total = order.shape[0]
    columns = query_weight.shape[1] + 3 * keyval_weight.shape[2] + LANES
    held = total // batches * columns // LANES
    whole = pl.BlockSpec(memory_space=pltpu.VMEM)
    return pl.pallas_call(
        project_kernel,
        out_shape=jax.ShapeDtypeStruct((batches, held, LANES), jnp.bfloat16),
        in_specs=[whole] * 6,
        out_specs=whole,
        compiler_params=pltpu.CompilerParams(vmem_limit_bytes=48 * MIB),
        cost_estimate=pl.CostEstimate(
            flops=2 * total * columns * gain.shape[0],
            bytes_accessed=2 * (gain.shape[0] + total) * columns,
            transcendentals=0,
        ),
        name="project_rows",
    )(order, parents, layer_input, gain.reshape(1, -1), query_weight, keyval_weight)


def gate_up_kernel(side, spans, order_ref, near_ref, far_ref, gain_ref, weight_ref, *refs):
    first_ref, second_refs = refs[0], refs[1 : 1 + side]
    held_ref, first_held, second_held, in_sems, first_sems, second_sems = refs[1 + side :]
    hidden = weight_ref.shape[2]
    loads = {}
    for half in (1, 0):
        for at, (start, size) in enumerate(spans):
            columns = pl.ds(start, size)
            loads[half, at] = pltpu.make_async_copy(
                weight_ref.at[half, :, columns],
                held_ref.at[half, :, columns],
                in_sems.at[half, at],
            )
    order = [(half, at) for half in (1, 0) for at in range(len(spans))]
    ahead = 4
    for key in order[:ahead]:
        loads[key].start()

    def arrived(half, at):
        step = order.index((half, at))
        if step + ahead < len(order):
            loads[order[step + ahead]].start()
        loads[half, at].wait()

    lifted = jnp.concatenate([near_ref[...], far_ref[...]], axis=0)
    ordered = dot(one_hot(order_ref[...], lifted.shape[0]), lifted)
    plain = ordered * (1.0 / gain_ref[...].astype(jnp.float32))
    statistics = in_lanes(split_pair(jnp.sum(plain * plain, axis=1, keepdims=True)))
    ordered = ordered.astype(jnp.bfloat16)
    rows = ordered.shape[0] // side
    stores = []
    for at, (start, size) in enumerate(spans):
        arrived(1, at)
        ups = dot(ordered, held_ref[1, :, start : start + size])
        for place in range(side):
            second_held[place, :, start : start + size] = ups[
                place * rows : (place + 1) * rows
            ].astype(jnp.bfloat16)
    for place in range(side):
        stores.append(
            pltpu.make_async_copy(
                second_held.at[place], second_refs[place], second_sems.at[place]
            )
        )
        stores[-1].start()
    for at, (start, size) in enumerate(list(spans) + [(hidden, LANES)]):
        if start < hidden:
            arrived(0, at)
            gates = dot(ordered, held_ref[0, :, start : start + size])
        else:
            gates = statistics
        for place in range(side):
            first_held[place, :, start : start + size] = blocks_along(gates, side, place).astype(
                jnp.bfloat16
            )
        columns = pl.ds(start, size)
        stores.append(
            pltpu.make_async_copy(
                first_held.at[:, :, columns], first_ref.at[:, :, columns], first_sems.at[at]
            )
        )
        stores[-1].start()
    for store in stores:
        store.wait()


def gate_up(side, order, near, far, gain, weight, tile):
    total, width = order.shape[0], near.shape[1]
    hidden = weight.shape[2]
    rows = total // side
    edges = [0] + list(range(hidden % tile or tile, hidden + 1, tile))
    spans = [(start, stop - start) for start, stop in zip(edges, edges[1:])]
    whole = pl.BlockSpec(memory_space=pltpu.VMEM)
    far_off = pl.BlockSpec(memory_space=pltpu.HBM)
    return pl.pallas_call(
        functools.partial(gate_up_kernel, side, spans),
        out_shape=[jax.ShapeDtypeStruct((side, rows, hidden + LANES), jnp.bfloat16)]
        + [jax.ShapeDtypeStruct((rows, hidden), jnp.bfloat16)] * side,
        in_specs=[whole] * 4 + [far_off],
        out_specs=[far_off] * (1 + side),
        scratch_shapes=[
            pltpu.VMEM(weight.shape, jnp.bfloat16),
            pltpu.VMEM((side, rows, hidden + LANES), jnp.bfloat16),
            pltpu.VMEM((side, rows, hidden), jnp.bfloat16),
            pltpu.SemaphoreType.DMA((2, len(spans))),
            pltpu.SemaphoreType.DMA((len(spans) + 1,)),
            pltpu.SemaphoreType.DMA((side,)),
        ],
        compiler_params=pltpu.CompilerParams(vmem_limit_bytes=58 * MIB),
        cost_estimate=pl.CostEstimate(
            flops=4 * total * width * hidden,
            bytes_accessed=4 * hidden * (width + total),
            transcendentals=0,
        ),
        name="gate_up",
    )(order, near, far, gain, weight)


def spread_dot_kernel(place_ref, rows_ref, weight_ref, kept_ref, sent_ref, total_ref):
    values = dot(rows_ref[...], weight_ref[...])
    blocks = place_ref.shape[0]
    rows = values.shape[0] // blocks
    for at in range(blocks):
        target = pl.ds(pl.multiple_of(place_ref[at], 8), rows)
        total_ref[target, :] = values[at * rows : (at + 1) * rows]
    half = kept_ref.shape[0]
    kept_ref[...] = total_ref[:half]
    sent_ref[...] = total_ref[half:].astype(jnp.bfloat16)


def spread_dot(places, values, weight):
    total, width = values.shape[0], weight.shape[1]
    whole = pl.BlockSpec(memory_space=pltpu.VMEM)
    return pl.pallas_call(
        spread_dot_kernel,
        out_shape=[
            jax.ShapeDtypeStruct((total // 2, width), kind) for kind in (jnp.float32, jnp.bfloat16)
        ],
        in_specs=[pl.BlockSpec(memory_space=pltpu.SMEM), whole, whole],
        out_specs=[whole] * 2,
        scratch_shapes=[pltpu.VMEM((total, width), jnp.float32)],
        compiler_params=pltpu.CompilerParams(vmem_limit_bytes=20 * MIB),
        cost_estimate=pl.CostEstimate(
            flops=2 * total * weight.size,
            bytes_accessed=2 * weight.size + 2 * total * (weight.shape[0] + 4 * width),
            transcendentals=0,
        ),
        name="spread_dot",
    )(places, values, weight)


def rotary(rows, first_position):
    inverse = np.exp(-math.log(rope_base) * np.arange(HD // 2, dtype=np.float64) * (2.0 / HD))
    angles = (first_position + np.repeat(np.arange(STEPS), rows))[:, None] * inverse[None, :]
    cosine, sine = np.cos(angles), np.sin(angles)
    return np.concatenate([cosine, cosine, -sine, sine], axis=1).astype(np.float32)


def attend_kernel(heads, rows, model, table_ref, cache_ref, *refs):
    out_ref, fresh_ref, kept_ref, query_ref, mix_ref, semaphores = refs
    total = STEPS * rows
    batches, span = kept_ref.shape[2:4]
    edge = (heads + 3) * HD
    stores = []
    for row in range(rows):
        for at in range(2):
            stores.append(
                pltpu.make_async_copy(
                    cache_ref.at[:, pl.ds((2 * (rows + row) + at) * span, span)],
                    kept_ref.at[at, row],
                    semaphores.at[at, row],
                )
            )
            stores[-1].start()
    parts = []
    for start in range(2 * total * span, cache_ref.shape[1], 2 * total):
        pair = cache_ref[0, start : start + 2 * total].astype(jnp.float32)
        for source in range(1, batches):
            pair = pair + cache_ref[source, start : start + 2 * total].astype(jnp.float32)
        parts += [pair[:total], pair[total:]]
    values = jnp.concatenate(parts, axis=1)
    cosine, sine = table_ref[:, :HD], table_ref[:, HD:]
    scale = lax.rsqrt((values[:, edge : edge + 1] + values[:, edge + 1 : edge + 2]) / model + norm_eps)
    parent_scale = lax.rsqrt(
        (values[:, edge + 2 : edge + 3] + values[:, edge + 3 : edge + 4]) / model + norm_eps
    )

    def rotate(block, cosine, sine):
        return block * cosine + pltpu.roll(block, HD // 2, 1) * sine

    def rounded(block):
        return block.astype(jnp.bfloat16).astype(jnp.float32)

    query_ref[...] = jnp.zeros(query_ref.shape, jnp.float32)
    for head in range(heads):
        block = values[:, head * HD : (head + 1) * HD] * scale
        query_ref[:, head, :] = rotate(block, cosine, sine)
    keys = rounded(rotate(values[:, heads * HD : (heads + 1) * HD] * scale, cosine, sine))
    news = rounded(values[:, (heads + 1) * HD : (heads + 2) * HD] * scale)
    parents = values[:, (heads + 2) * HD : edge] * parent_scale
    parent_keys = rounded(rotate(parents[:rows], cosine[:rows], sine[:rows]))
    parent_news = rounded(parents[rows:])
    fresh_ref[0] = jnp.concatenate([keys[:rows], parent_keys], axis=0)
    fresh_ref[1] = keys
    fresh_ref[2] = jnp.concatenate([news[:rows], parent_news], axis=0)
    fresh_ref[3] = news
    queries = query_ref[...].astype(jnp.bfloat16)
    wide = queries.astype(jnp.float32)
    scores = jnp.concatenate(
        [
            lax.dot_general(
                queries[row],
                cache_ref[:, 2 * row * span : (2 * row + 1) * span].reshape(-1, HD),
                (((1,), (1,)), ((), ())),
                preferred_element_type=jnp.float32,
            )
            for row in range(total)
        ],
        axis=0,
    ).reshape(total, queries.shape[1], -1) * (1.0 / math.sqrt(HD))
    extra = [
        jnp.sum(wide * fresh_ref[at][:, None, :], axis=2, keepdims=True) * (1.0 / math.sqrt(HD))
        for at in range(STEPS)
    ]
    later = lax.broadcasted_iota(jnp.int32, extra[1].shape, 0) >= rows
    extra[1] = jnp.where(later, extra[1], -jnp.inf)
    top = jnp.maximum(
        jnp.max(scores, axis=2, keepdims=True), jnp.maximum(extra[0], extra[1])
    )
    weights = jnp.exp(scores - top)
    extra = [jnp.exp(score - top) for score in extra]
    whole = jnp.sum(weights, axis=2, keepdims=True) + extra[0] + extra[1]
    weights = (weights / whole).astype(jnp.bfloat16)
    extra = [rounded(weight / whole) for weight in extra]
    for row in range(total):
        mix_ref[row] = dot(weights[row], cache_ref[:, (2 * row + 1) * span : (2 * row + 2) * span].reshape(-1, HD))
    mix_ref[...] = (
        mix_ref[...]
        + extra[0] * fresh_ref[2][:, None, :]
        + extra[1] * fresh_ref[3][:, None, :]
    )
    for head in range(heads):
        block = mix_ref[:, head, :].astype(jnp.bfloat16)
        for copy in range(out_ref.shape[0]):
            out_ref[copy, :, head * HD : (head + 1) * HD] = block
    for store in stores:
        store.wait()


def attend(returned, heads, rows, past, model):
    batches, total = returned.shape[0], STEPS * rows
    padded = -(-heads // 8) * 8
    whole = pl.BlockSpec(memory_space=pltpu.VMEM)
    return pl.pallas_call(
        functools.partial(attend_kernel, heads, rows, model),
        out_shape=[
            jax.ShapeDtypeStruct((batches, total, heads * HD), jnp.bfloat16),
            jax.ShapeDtypeStruct((2 * STEPS, total, HD), jnp.float32),
            jax.ShapeDtypeStruct((2, rows, batches, past // batches, HD), jnp.bfloat16),
        ],
        grid=(1,),
        in_specs=[whole, pl.BlockSpec(returned.shape, lambda step: (0, 0, 0))],
        out_specs=[whole] * 2 + [pl.BlockSpec(memory_space=pl.ANY)],
        scratch_shapes=[pltpu.VMEM((total, padded, HD), jnp.float32)] * 2
        + [pltpu.SemaphoreType.DMA((2, rows))],
        compiler_params=pltpu.CompilerParams(vmem_limit_bytes=48 * MIB),
        cost_estimate=pl.CostEstimate(
            flops=4 * total * padded * past * HD,
            bytes_accessed=4 * returned.size,
            transcendentals=total * padded * past,
        ),
        name="attend",
    )(jnp.asarray(rotary(rows, past)), returned)


def pick_kernel(index_ref, table_ref, sum_ref, out_ref):
    span = table_ref.shape[1]
    count = index_ref.shape[0] // out_ref.shape[0]

    @pl.loop(0, out_ref.shape[0])
    def _(block):
        for row in range(count):
            out_ref[block, row * span : (row + 1) * span] = table_ref[
                index_ref[block * count + row]
            ]
        out_ref[block, count * span :] = sum_ref[block]


def pick_rows(table, index, sums):
    batches, held, _ = sums.shape
    count = index.shape[0] // batches * table.shape[1]
    whole = pl.BlockSpec(memory_space=pltpu.VMEM)
    return pl.pallas_call(
        pick_kernel,
        out_shape=jax.ShapeDtypeStruct((batches, count + held, LANES), table.dtype),
        in_specs=[pl.BlockSpec(memory_space=pltpu.SMEM), whole, whole],
        out_specs=whole,
        compiler_params=pltpu.CompilerParams(vmem_limit_bytes=32 * MIB),
        cost_estimate=pl.CostEstimate(
            flops=0, bytes_accessed=4 * batches * (count + held) * LANES, transcendentals=0
        ),
        name="pick_rows",
    )(index, table, sums)


def on_device(
    layer_input,
    attn_gain,
    ffn_gain,
    query_weight,
    keyval_weight,
    output_weight,
    gateup_weight,
    down_weight,
    past_cache,
    parent_rows,
):
    batches = lax.axis_size("batch")
    tensors = lax.axis_size("tensor")
    side = math.isqrt(batches)
    chips = tensors // 2
    batch_index = lax.axis_index("batch")
    tensor_index = lax.axis_index("tensor")
    my_major = batch_index // side
    my_chip, my_core = tensor_index // 2, tensor_index % 2
    _, rows, past, kv_width = past_cache.shape
    width = layer_input.shape[2]
    model = width * batches
    head_width = query_weight.shape[1]
    heads = head_width // HD
    hidden = gateup_weight.shape[2]
    both = STEPS * rows
    total = batches * both
    share = total // tensors
    span = past // batches

    with jax.named_scope("cache_spread"):
        pieces = past_cache.reshape(2, rows, batches, span, kv_width).transpose(2, 1, 0, 3, 4)
        spread = exchange(pieces, "batch").reshape(batches * rows, 2 * span, kv_width)

    with jax.named_scope("places"):
        parents = parent_rows.reshape(STEPS, batches, rows)
        origin = jnp.take(parent_rows[0], parent_rows[1], axis=0)
        wanted = jnp.stack([parents[0], origin.reshape(batches, rows)], axis=1).reshape(total)
        place = jnp.arange(total, dtype=jnp.int32)
        inner = place % both
        near = place // both
        input_order = ((inner // rows) * (batches * rows) + near * rows + inner % rows)[:, None]
        row = (my_major + place // (side * both)) % side * side + place // both % side
        row = row * both + inner
        owner = row // share
        lifted_order = (owner % 2 != my_core).astype(jnp.int32) * (total // 2)
        lifted_order = lifted_order + (my_chip - owner // 2 + chips) % chips * share
        lifted_order = (lifted_order + row % share)[:, None]
        block = jnp.arange(batches, dtype=jnp.int32)
        owner = block * both // share
        targets = (owner % 2 != my_core).astype(jnp.int32) * (total // 2)
        targets = targets + (owner // 2 - my_chip + chips) % chips * share
        targets = targets + block * both % share

    with jax.named_scope("project"):
        sums = project_rows(
            batches,
            input_order,
            parent_rows[1][:, None],
            after(layer_input, pieces),
            attn_gain,
            query_weight,
            keyval_weight,
        )

    with jax.named_scope("cache_return"):
        lift_gain = ffn_gain.reshape(1, -1)
        ready = after(wanted, (lifted_order, targets, lift_gain))
        returned = exchange(pick_rows(spread, ready, sums), "batch")

    with jax.named_scope("attention"):
        attended, fresh, kept = attend(returned, heads, rows, past, model)
        fresh_out = fresh.reshape(2, STEPS, both, kv_width)[:, :, rows:].transpose(0, 2, 1, 3)
        fresh_out = fresh_out.astype(jnp.bfloat16)
        cache_out = kept.reshape(2, rows, past, kv_width)
        attended = exchange(attended, "batch").reshape(total, head_width)

    with jax.named_scope("output_projection"):
        own_inputs = lax.dynamic_slice_in_dim(
            layer_input, tensor_index * (share // STEPS), share // STEPS, 1
        )
        own_inputs = (
            own_inputs.reshape(STEPS, share // both, rows, width)
            .transpose(1, 0, 2, 3)
            .reshape(share, width)
        )
        mixed = add_over_tensor(*spread_dot(targets, attended, output_weight))
        residual = own_inputs.astype(jnp.float32) + mixed
        lifted = (residual * ffn_gain.astype(jnp.float32)).astype(jnp.bfloat16)
        near = jnp.concatenate(
            [lifted] + [shift_chips(lifted, count) for count in range(1, chips)], axis=0
        )
        far = swap_cores(near)

    with jax.named_scope("gate_up"):
        blocks = gate_up(side, lifted_order, near, far, lift_gain, gateup_weight, 768)
        gates, terms, ups = add_crossed(blocks[0], blocks[1:])
        activated = activate(gates, terms, ups, model, batches)
        activated = exchange(activated, "batch").reshape(total, hidden)

    with jax.named_scope("down_projection"):
        lowered = add_over_tensor(*spread_dot(targets, activated, down_weight))
        final = (residual + lowered).astype(jnp.bfloat16)
        layer_out = (
            final.reshape(share // both, STEPS, rows, width)
            .transpose(1, 0, 2, 3)
            .reshape(STEPS, share // STEPS, width)
        )
    return layer_out, cache_out, fresh_out


def solution(mesh):
    return jax.shard_map(
        on_device,
        mesh=mesh,
        in_specs=(
            P(None, None, "batch"),
            P("batch"),
            P("batch"),
            P("batch", "tensor"),
            P(None, "batch", "tensor"),
            P("tensor", "batch"),
            P(None, "batch", "tensor"),
            P("tensor", "batch"),
            P(None, "batch", None, "tensor"),
            P(),
        ),
        out_specs=(
            P(None, "tensor", "batch"),
            P(None, "batch", None, "tensor"),
            P(None, "batch", None, "tensor"),
        ),
        check_vma=False,
    )
```

```python
import functools
import math

import jax
import jax.numpy as jnp
import numpy as np
from jax import lax
from jax.experimental import pallas as pl
from jax.experimental.pallas import tpu as pltpu
from jax.sharding import PartitionSpec as P

HD = 128
LANES = 128
STEPS = 2
MIB = 1024 * 1024

rope_base = 1000000.0
norm_eps = 1e-05


def exchange(blocks, axis):
    return lax.all_to_all(blocks, axis, split_axis=0, concat_axis=0, tiled=True)


def after(value, earlier):
    return lax.optimization_barrier((value, earlier))[0]


def shift_along(block, minor_axis, count):
    side = math.isqrt(lax.axis_size("batch"))
    pairs = []
    for major in range(side):
        for minor in range(side):
            target = (
                (major, (minor + count) % side) if minor_axis else ((major + count) % side, minor)
            )
            pairs.append((major * side + minor, target[0] * side + target[1]))
    return lax.ppermute(block, "batch", pairs)


def shift_chips(block, count):
    size = lax.axis_size("tensor")
    return lax.ppermute(block, "tensor", [(at, (at + 2 * count) % size) for at in range(size)])


def swap_cores(block):
    size = lax.axis_size("tensor")
    return lax.ppermute(block, "tensor", [(at, at ^ 1) for at in range(size)])


def fold_kernel(count, *refs):
    sources, targets = refs[:count], refs[count:]
    terms = []
    for source in sources:
        terms += [source] if len(source.shape) == 2 else [source.at[at] for at in range(source.shape[0])]
    total = terms[0][...].astype(jnp.float32)
    for term in terms[1:]:
        total = total + term[...].astype(jnp.float32)
    rows = total.shape[0] // len(targets)
    for place, target in enumerate(targets):
        target[...] = total[place * rows : (place + 1) * rows].astype(target.dtype)


def fold(sources, pieces):
    rows, columns = sources[0].shape[-2:]
    kinds = [jnp.float32] + [jnp.bfloat16] * (pieces - 1)
    whole = pl.BlockSpec(memory_space=pltpu.VMEM)
    return pl.pallas_call(
        functools.partial(fold_kernel, len(sources)),
        out_shape=[jax.ShapeDtypeStruct((rows // pieces, columns), kind) for kind in kinds],
        in_specs=[whole] * len(sources),
        out_specs=[whole] * pieces,
        compiler_params=pltpu.CompilerParams(vmem_limit_bytes=32 * MIB),
        cost_estimate=pl.CostEstimate(flops=1, bytes_accessed=1, transcendentals=0),
        name="fold",
    )(*sources)


def exchange_minor(blocks):
    side = math.isqrt(lax.axis_size("batch"))
    groups = [[major * side + minor for minor in range(side)] for major in range(side)]
    return lax.all_to_all(
        blocks, "batch", split_axis=0, concat_axis=0, tiled=True, axis_index_groups=groups
    )


def exchange_minor(blocks):
    side = math.isqrt(lax.axis_size("batch"))
    groups = [[major * side + minor for minor in range(side)] for major in range(side)]
    return lax.all_to_all(
        blocks, "batch", split_axis=0, concat_axis=0, tiled=True, axis_index_groups=groups
    )


def add_along(own, terms):
    return functools.reduce(lambda total, term: total + term.astype(jnp.float32), terms, own)


def stack_kernel(*refs):
    sources, target = refs[:-1], refs[-1]
    total = sources[0][...].astype(jnp.float32)
    for source in sources[1:]:
        total = total + source[...].astype(jnp.float32)
    rows = target.shape[1]
    for place in range(target.shape[0]):
        target[place] = total[place * rows : (place + 1) * rows].astype(target.dtype)


def fold_stacked(sources):
    rows, columns = sources[0].shape
    shape = (len(sources), rows // len(sources), columns)
    whole = pl.BlockSpec(memory_space=pltpu.VMEM)
    return pl.pallas_call(
        stack_kernel,
        out_shape=jax.ShapeDtypeStruct(shape, jnp.bfloat16),
        in_specs=[whole] * len(sources),
        out_specs=whole,
        compiler_params=pltpu.CompilerParams(vmem_limit_bytes=32 * MIB),
        cost_estimate=pl.CostEstimate(flops=1, bytes_accessed=1, transcendentals=0),
        name="fold_stacked",
    )(*sources)


def activate_kernel(model, own_ref, *refs):
    terms, crossed_ref, out_ref = refs[:-2], refs[-2], refs[-1]
    hidden = out_ref.shape[2]
    gates = own_ref[...]
    for term in terms:
        gates = gates + term[...].astype(jnp.float32)
    ups = crossed_ref[0].astype(jnp.float32)
    for place in range(1, crossed_ref.shape[0]):
        ups = ups + crossed_ref[place].astype(jnp.float32)
    mean = (gates[:, hidden : hidden + 1] + gates[:, hidden + 1 : hidden + 2]) / model
    scale = lax.rsqrt(mean + norm_eps)
    gates, ups = gates[:, :hidden] * scale, ups * scale
    activated = (gates / (1.0 + jnp.exp(-gates)) * ups).astype(jnp.bfloat16)
    for copy in range(out_ref.shape[0]):
        out_ref[copy] = activated


def activate(own, terms, crossed, model, copies):
    _, rows, hidden = crossed.shape
    whole = pl.BlockSpec(memory_space=pltpu.VMEM)
    return pl.pallas_call(
        functools.partial(activate_kernel, model),
        out_shape=jax.ShapeDtypeStruct((copies, rows, hidden), jnp.bfloat16),
        in_specs=[whole] * (2 + len(terms)),
        out_specs=whole,
        compiler_params=pltpu.CompilerParams(vmem_limit_bytes=32 * MIB),
        cost_estimate=pl.CostEstimate(
            flops=8 * rows * hidden,
            bytes_accessed=2 * copies * rows * hidden,
            transcendentals=rows * hidden,
        ),
        name="activate",
    )(own, *terms, crossed)


def add_crossed(first, second):
    side = len(second)
    others = range(1, side)
    moved = [second[0]] + [shift_along(second[count], 0, count) for count in others]
    summed = fold([exchange_minor(first)], side)
    terms = [shift_along(summed[count], 0, count) for count in others]
    return summed[0], terms, exchange_minor(fold_stacked(moved))


def add_over_tensor(kept, sent):
    chips = lax.axis_size("tensor") // 2
    pieces = fold([kept, swap_cores(sent)], chips)
    total = pieces[0]
    for count in range(1, chips):
        total = total + shift_chips(pieces[count], count).astype(jnp.float32)
    return total


def blocks_along(values, side, place):
    rows = values.shape[0] // (side * side)
    return jnp.concatenate(
        [
            values[(major * side + place) * rows : (major * side + place + 1) * rows]
            for major in range(side)
        ],
        axis=0,
    )


def one_hot(index, count):
    places = lax.broadcasted_iota(jnp.int32, (index.shape[0], count), 1)
    return jnp.where(places == index, 1.0, 0.0).astype(jnp.bfloat16)


def dot(left, right):
    return jnp.dot(left, right, preferred_element_type=jnp.float32)


def split_pair(values):
    high = values.astype(jnp.bfloat16).astype(jnp.float32)
    return [high, values - high]


def in_lanes(columns):
    lanes = lax.broadcasted_iota(jnp.int32, (columns[0].shape[0], LANES), 1)
    packed = jnp.zeros(lanes.shape, jnp.float32)
    for place, value in enumerate(columns):
        packed = jnp.where(lanes == place, value, packed)
    return packed


def project_kernel(
    order_ref, parent_ref, input_ref, gain_ref, query_ref, keyval_ref, out_ref
):
    steps, count, width = input_ref.shape
    source = input_ref[...].reshape(steps * count, width)
    gain = gain_ref[...].astype(jnp.float32)
    order = order_ref[...]
    is_key = order < count
    own = dot(one_hot(order, steps * count), source)
    parents = dot(one_hot(parent_ref[...], count), input_ref[0]).astype(jnp.bfloat16)
    parents = dot(one_hot(jnp.where(is_key, order, order - count), count), parents)
    statistics = split_pair(jnp.sum(own * own, axis=1, keepdims=True)) + split_pair(
        jnp.sum(parents * parents, axis=1, keepdims=True)
    )
    own = (own * gain).astype(jnp.bfloat16)
    parents = (parents * gain).astype(jnp.bfloat16)
    values = jnp.concatenate(
        [
            dot(own, query_ref[...]),
            dot(own, keyval_ref[0]),
            dot(own, keyval_ref[1]),
            jnp.where(is_key, dot(parents, keyval_ref[0]), dot(parents, keyval_ref[1])),
            in_lanes(statistics),
        ],
        axis=1,
    ).astype(jnp.float32)
    blocks, held, _ = out_ref.shape
    rows = values.shape[0] // blocks
    for block in range(blocks):
        part = values[block * rows : (block + 1) * rows]
        for at in range(held // (2 * rows)):
            pair = [
                part[:, (2 * at + side) * LANES : (2 * at + side + 1) * LANES] for side in range(2)
            ]
            out_ref[block, 2 * at * rows : 2 * (at + 1) * rows] = jnp.concatenate(
                pair, axis=0
            ).astype(jnp.bfloat16)


def project_rows(batches, order, parents, layer_input, gain, query_weight, keyval_weight):
    total = order.shape[0]
    columns = query_weight.shape[1] + 3 * keyval_weight.shape[2] + LANES
    held = total // batches * columns // LANES
    whole = pl.BlockSpec(memory_space=pltpu.VMEM)
    return pl.pallas_call(
        project_kernel,
        out_shape=jax.ShapeDtypeStruct((batches, held, LANES), jnp.bfloat16),
        in_specs=[whole] * 6,
        out_specs=whole,
        compiler_params=pltpu.CompilerParams(vmem_limit_bytes=48 * MIB),
        cost_estimate=pl.CostEstimate(
            flops=2 * total * columns * gain.shape[0],
            bytes_accessed=2 * (gain.shape[0] + total) * columns,
            transcendentals=0,
        ),
        name="project_rows",
    )(order, parents, layer_input, gain.reshape(1, -1), query_weight, keyval_weight)


def gate_up_kernel(side, spans, order_ref, near_ref, far_ref, gain_ref, weight_ref, *refs):
    first_ref, second_refs = refs[0], refs[1 : 1 + side]
    held_ref, first_held, second_held, in_sems, first_sems, second_sems = refs[1 + side :]
    hidden = weight_ref.shape[2]
    loads = {}
    for half in (1, 0):
        for at, (start, size) in enumerate(spans):
            columns = pl.ds(start, size)
            loads[half, at] = pltpu.make_async_copy(
                weight_ref.at[half, :, columns],
                held_ref.at[half, :, columns],
                in_sems.at[half, at],
            )
    order = [(half, at) for half in (1, 0) for at in (range(len(spans)) if half else reversed(range(len(spans))))]
    ahead = 4
    for key in order[:ahead]:
        loads[key].start()

    def arrived(half, at):
        step = order.index((half, at))
        if step + ahead < len(order):
            loads[order[step + ahead]].start()
        loads[half, at].wait()

    lifted = jnp.concatenate([near_ref[...], far_ref[...]], axis=0)
    ordered = dot(one_hot(order_ref[...], lifted.shape[0]), lifted)
    plain = ordered * (1.0 / gain_ref[...].astype(jnp.float32))
    statistics = in_lanes(split_pair(jnp.sum(plain * plain, axis=1, keepdims=True)))
    ordered = ordered.astype(jnp.bfloat16)
    rows = ordered.shape[0] // side
    stores = []
    for at, (start, size) in enumerate(spans):
        arrived(1, at)
        ups = dot(ordered, held_ref[1, :, start : start + size])
        for place in range(side):
            second_held[place, :, start : start + size] = ups[
                place * rows : (place + 1) * rows
            ].astype(jnp.bfloat16)
    for place in range(side):
        stores.append(
            pltpu.make_async_copy(
                second_held.at[place], second_refs[place], second_sems.at[place]
            )
        )
        stores[-1].start()
    for at, (start, size) in reversed(list(enumerate(list(spans) + [(hidden, LANES)]))):
        if start < hidden:
            arrived(0, at)
            gates = dot(ordered, held_ref[0, :, start : start + size])
        else:
            gates = statistics
        for place in range(side):
            first_held[place, :, start : start + size] = blocks_along(gates, side, place).astype(
                jnp.bfloat16
            )
        columns = pl.ds(start, size)
        stores.append(
            pltpu.make_async_copy(
                first_held.at[:, :, columns], first_ref.at[:, :, columns], first_sems.at[at]
            )
        )
        stores[-1].start()
    for store in stores:
        store.wait()


def gate_up(side, order, near, far, gain, weight, tile):
    total, width = order.shape[0], near.shape[1]
    hidden = weight.shape[2]
    rows = total // side
    edges = [0] + list(range(hidden % tile or tile, hidden + 1, tile))
    spans = [(start, stop - start) for start, stop in zip(edges, edges[1:])]
    whole = pl.BlockSpec(memory_space=pltpu.VMEM)
    far_off = pl.BlockSpec(memory_space=pltpu.HBM)
    return pl.pallas_call(
        functools.partial(gate_up_kernel, side, spans),
        out_shape=[jax.ShapeDtypeStruct((side, rows, hidden + LANES), jnp.bfloat16)]
        + [jax.ShapeDtypeStruct((rows, hidden), jnp.bfloat16)] * side,
        in_specs=[whole] * 4 + [far_off],
        out_specs=[far_off] * (1 + side),
        scratch_shapes=[
            pltpu.VMEM(weight.shape, jnp.bfloat16),
            pltpu.VMEM((side, rows, hidden + LANES), jnp.bfloat16),
            pltpu.VMEM((side, rows, hidden), jnp.bfloat16),
            pltpu.SemaphoreType.DMA((2, len(spans))),
            pltpu.SemaphoreType.DMA((len(spans) + 1,)),
            pltpu.SemaphoreType.DMA((side,)),
        ],
        compiler_params=pltpu.CompilerParams(vmem_limit_bytes=58 * MIB),
        cost_estimate=pl.CostEstimate(
            flops=4 * total * width * hidden,
            bytes_accessed=4 * hidden * (width + total),
            transcendentals=0,
        ),
        name="gate_up",
    )(order, near, far, gain, weight)


def spread_dot_kernel(place_ref, rows_ref, weight_ref, kept_ref, sent_ref, total_ref):
    values = dot(rows_ref[...], weight_ref[...])
    blocks = place_ref.shape[0]
    rows = values.shape[0] // blocks
    for at in range(blocks):
        target = pl.ds(pl.multiple_of(place_ref[at], 8), rows)
        total_ref[target, :] = values[at * rows : (at + 1) * rows]
    half = kept_ref.shape[0]
    kept_ref[...] = total_ref[:half]
    sent_ref[...] = total_ref[half:].astype(jnp.bfloat16)


def spread_dot(places, values, weight):
    total, width = values.shape[0], weight.shape[1]
    whole = pl.BlockSpec(memory_space=pltpu.VMEM)
    return pl.pallas_call(
        spread_dot_kernel,
        out_shape=[
            jax.ShapeDtypeStruct((total // 2, width), kind) for kind in (jnp.float32, jnp.bfloat16)
        ],
        in_specs=[pl.BlockSpec(memory_space=pltpu.SMEM), whole, whole],
        out_specs=[whole] * 2,
        scratch_shapes=[pltpu.VMEM((total, width), jnp.float32)],
        compiler_params=pltpu.CompilerParams(vmem_limit_bytes=20 * MIB),
        cost_estimate=pl.CostEstimate(
            flops=2 * total * weight.size,
            bytes_accessed=2 * weight.size + 2 * total * (weight.shape[0] + 4 * width),
            transcendentals=0,
        ),
        name="spread_dot",
    )(places, values, weight)


def rotary(rows, first_position):
    inverse = np.exp(-math.log(rope_base) * np.arange(HD // 2, dtype=np.float64) * (2.0 / HD))
    angles = (first_position + np.repeat(np.arange(STEPS), rows))[:, None] * inverse[None, :]
    cosine, sine = np.cos(angles), np.sin(angles)
    return np.concatenate([cosine, cosine, -sine, sine], axis=1).astype(np.float32)


def attend_kernel(heads, rows, model, table_ref, cache_ref, *refs):
    out_ref, fresh_ref, kept_ref, query_ref, mix_ref, semaphores = refs
    total = STEPS * rows
    batches, span = kept_ref.shape[2:4]
    edge = (heads + 3) * HD
    stores = []
    for row in range(rows):
        for at in range(2):
            stores.append(
                pltpu.make_async_copy(
                    cache_ref.at[:, pl.ds((2 * (rows + row) + at) * span, span)],
                    kept_ref.at[at, row],
                    semaphores.at[at, row],
                )
            )
            stores[-1].start()
    parts = []
    for start in range(2 * total * span, cache_ref.shape[1], 2 * total):
        pair = cache_ref[0, start : start + 2 * total].astype(jnp.float32)
        for source in range(1, batches):
            pair = pair + cache_ref[source, start : start + 2 * total].astype(jnp.float32)
        parts += [pair[:total], pair[total:]]
    values = jnp.concatenate(parts, axis=1)
    cosine, sine = table_ref[:, :HD], table_ref[:, HD:]
    scale = lax.rsqrt((values[:, edge : edge + 1] + values[:, edge + 1 : edge + 2]) / model + norm_eps)
    parent_scale = lax.rsqrt(
        (values[:, edge + 2 : edge + 3] + values[:, edge + 3 : edge + 4]) / model + norm_eps
    )

    def rotate(block, cosine, sine):
        return block * cosine + pltpu.roll(block, HD // 2, 1) * sine

    def rounded(block):
        return block.astype(jnp.bfloat16).astype(jnp.float32)

    query_ref[...] = jnp.zeros(query_ref.shape, jnp.float32)
    for head in range(heads):
        block = values[:, head * HD : (head + 1) * HD] * scale
        query_ref[:, head, :] = rotate(block, cosine, sine)
    keys = rounded(rotate(values[:, heads * HD : (heads + 1) * HD] * scale, cosine, sine))
    news = rounded(values[:, (heads + 1) * HD : (heads + 2) * HD] * scale)
    parents = values[:, (heads + 2) * HD : edge] * parent_scale
    parent_keys = rounded(rotate(parents[:rows], cosine[:rows], sine[:rows]))
    parent_news = rounded(parents[rows:])
    fresh_ref[0] = jnp.concatenate([keys[:rows], parent_keys], axis=0)
    fresh_ref[1] = keys
    fresh_ref[2] = jnp.concatenate([news[:rows], parent_news], axis=0)
    fresh_ref[3] = news
    queries = query_ref[...].astype(jnp.bfloat16)
    wide = queries.astype(jnp.float32)
    scores = jnp.concatenate(
        [
            lax.dot_general(
                queries[row],
                cache_ref[:, 2 * row * span : (2 * row + 1) * span].reshape(-1, HD),
                (((1,), (1,)), ((), ())),
                preferred_element_type=jnp.float32,
            )
            for row in range(total)
        ],
        axis=0,
    ).reshape(total, queries.shape[1], -1) * (1.0 / math.sqrt(HD))
    extra = [
        jnp.sum(wide * fresh_ref[at][:, None, :], axis=2, keepdims=True) * (1.0 / math.sqrt(HD))
        for at in range(STEPS)
    ]
    later = lax.broadcasted_iota(jnp.int32, extra[1].shape, 0) >= rows
    extra[1] = jnp.where(later, extra[1], -jnp.inf)
    top = jnp.maximum(
        jnp.max(scores, axis=2, keepdims=True), jnp.maximum(extra[0], extra[1])
    )
    weights = jnp.exp(scores - top)
    extra = [jnp.exp(score - top) for score in extra]
    whole = jnp.sum(weights, axis=2, keepdims=True) + extra[0] + extra[1]
    weights = (weights / whole).astype(jnp.bfloat16)
    extra = [rounded(weight / whole) for weight in extra]
    for row in range(total):
        mix_ref[row] = dot(weights[row], cache_ref[:, (2 * row + 1) * span : (2 * row + 2) * span].reshape(-1, HD))
    mix_ref[...] = (
        mix_ref[...]
        + extra[0] * fresh_ref[2][:, None, :]
        + extra[1] * fresh_ref[3][:, None, :]
    )
    for head in range(heads):
        block = mix_ref[:, head, :].astype(jnp.bfloat16)
        for copy in range(out_ref.shape[0]):
            out_ref[copy, :, head * HD : (head + 1) * HD] = block
    for store in stores:
        store.wait()


def attend(returned, heads, rows, past, model):
    batches, total = returned.shape[0], STEPS * rows
    padded = -(-heads // 8) * 8
    whole = pl.BlockSpec(memory_space=pltpu.VMEM)
    return pl.pallas_call(
        functools.partial(attend_kernel, heads, rows, model),
        out_shape=[
            jax.ShapeDtypeStruct((batches, total, heads * HD), jnp.bfloat16),
            jax.ShapeDtypeStruct((2 * STEPS, total, HD), jnp.float32),
            jax.ShapeDtypeStruct((2, rows, batches, past // batches, HD), jnp.bfloat16),
        ],
        grid=(1,),
        in_specs=[whole, pl.BlockSpec(returned.shape, lambda step: (0, 0, 0))],
        out_specs=[whole] * 2 + [pl.BlockSpec(memory_space=pl.ANY)],
        scratch_shapes=[pltpu.VMEM((total, padded, HD), jnp.float32)] * 2
        + [pltpu.SemaphoreType.DMA((2, rows))],
        compiler_params=pltpu.CompilerParams(vmem_limit_bytes=48 * MIB),
        cost_estimate=pl.CostEstimate(
            flops=4 * total * padded * past * HD,
            bytes_accessed=4 * returned.size,
            transcendentals=total * padded * past,
        ),
        name="attend",
    )(jnp.asarray(rotary(rows, past)), returned)


def cut_kernel(cache_ref, out_ref):
    blocks, rows, halves, span, _ = out_ref.shape
    for block in range(blocks):
        for half in range(halves):
            out_ref[block, :, half] = cache_ref[half, :, block * span : (block + 1) * span]


def cut_positions(cache, blocks):
    halves, rows, past, width = cache.shape
    shape = (blocks, rows, halves, past // blocks, width)
    whole = pl.BlockSpec(memory_space=pltpu.VMEM)
    return pl.pallas_call(
        cut_kernel,
        out_shape=jax.ShapeDtypeStruct(shape, cache.dtype),
        in_specs=[whole],
        out_specs=whole,
        compiler_params=pltpu.CompilerParams(vmem_limit_bytes=58 * MIB),
        cost_estimate=pl.CostEstimate(
            flops=0, bytes_accessed=4 * cache.size, transcendentals=0
        ),
        name="cut_positions",
    )(cache)


def pick_kernel(index_ref, table_ref, sum_ref, out_ref):
    span = table_ref.shape[1]
    count = index_ref.shape[0] // out_ref.shape[0]

    @pl.loop(0, out_ref.shape[0])
    def _(block):
        for row in range(count):
            out_ref[block, row * span : (row + 1) * span] = table_ref[
                index_ref[block * count + row]
            ]
        out_ref[block, count * span :] = sum_ref[block]


def pick_rows(table, index, sums):
    batches, held, _ = sums.shape
    count = index.shape[0] // batches * table.shape[1]
    whole = pl.BlockSpec(memory_space=pltpu.VMEM)
    return pl.pallas_call(
        pick_kernel,
        out_shape=jax.ShapeDtypeStruct((batches, count + held, LANES), table.dtype),
        in_specs=[pl.BlockSpec(memory_space=pltpu.SMEM), whole, whole],
        out_specs=whole,
        compiler_params=pltpu.CompilerParams(vmem_limit_bytes=32 * MIB),
        cost_estimate=pl.CostEstimate(
            flops=0, bytes_accessed=4 * batches * (count + held) * LANES, transcendentals=0
        ),
        name="pick_rows",
    )(index, table, sums)


def on_device(
    layer_input,
    attn_gain,
    ffn_gain,
    query_weight,
    keyval_weight,
    output_weight,
    gateup_weight,
    down_weight,
    past_cache,
    parent_rows,
):
    batches = lax.axis_size("batch")
    tensors = lax.axis_size("tensor")
    side = math.isqrt(batches)
    chips = tensors // 2
    batch_index = lax.axis_index("batch")
    tensor_index = lax.axis_index("tensor")
    my_major = batch_index // side
    my_chip, my_core = tensor_index // 2, tensor_index % 2
    _, rows, past, kv_width = past_cache.shape
    width = layer_input.shape[2]
    model = width * batches
    head_width = query_weight.shape[1]
    heads = head_width // HD
    hidden = gateup_weight.shape[2]
    both = STEPS * rows
    total = batches * both
    share = total // tensors
    span = past // batches

    with jax.named_scope("cache_spread"):
        pieces = cut_positions(past_cache, batches)
        spread = exchange(pieces, "batch").reshape(batches * rows, 2 * span, kv_width)

    with jax.named_scope("places"):
        parents = parent_rows.reshape(STEPS, batches, rows)
        origin = jnp.take(parent_rows[0], parent_rows[1], axis=0)
        wanted = jnp.stack([parents[0], origin.reshape(batches, rows)], axis=1).reshape(total)
        place = jnp.arange(total, dtype=jnp.int32)
        inner = place % both
        near = place // both
        input_order = ((inner // rows) * (batches * rows) + near * rows + inner % rows)[:, None]
        row = (my_major + place // (side * both)) % side * side + place // both % side
        row = row * both + inner
        owner = row // share
        lifted_order = (owner % 2 != my_core).astype(jnp.int32) * (total // 2)
        lifted_order = lifted_order + (my_chip - owner // 2 + chips) % chips * share
        lifted_order = (lifted_order + row % share)[:, None]
        block = jnp.arange(batches, dtype=jnp.int32)
        owner = block * both // share
        targets = (owner % 2 != my_core).astype(jnp.int32) * (total // 2)
        targets = targets + (owner // 2 - my_chip + chips) % chips * share
        targets = targets + block * both % share

    with jax.named_scope("project"):
        sums = project_rows(
            batches,
            input_order,
            parent_rows[1][:, None],
            after(layer_input, pieces),
            attn_gain,
            query_weight,
            keyval_weight,
        )

    with jax.named_scope("cache_return"):
        lift_gain = ffn_gain.reshape(1, -1)
        ready = after(wanted, (lifted_order, targets, lift_gain))
        returned = exchange(pick_rows(spread, ready, sums), "batch")

    with jax.named_scope("attention"):
        attended, fresh, kept = attend(returned, heads, rows, past, model)
        fresh_out = fresh.reshape(2, STEPS, both, kv_width)[:, :, rows:].transpose(0, 2, 1, 3)
        fresh_out = fresh_out.astype(jnp.bfloat16)
        cache_out = kept.reshape(2, rows, past, kv_width)
        attended = exchange(attended, "batch").reshape(total, head_width)

    with jax.named_scope("output_projection"):
        own_inputs = lax.dynamic_slice_in_dim(
            layer_input, tensor_index * (share // STEPS), share // STEPS, 1
        )
        own_inputs = (
            own_inputs.reshape(STEPS, share // both, rows, width)
            .transpose(1, 0, 2, 3)
            .reshape(share, width)
        )
        mixed = add_over_tensor(*spread_dot(targets, attended, output_weight))
        residual = own_inputs.astype(jnp.float32) + mixed
        lifted = (residual * ffn_gain.astype(jnp.float32)).astype(jnp.bfloat16)
        near = jnp.concatenate(
            [lifted] + [shift_chips(lifted, count) for count in range(1, chips)], axis=0
        )
        far = swap_cores(near)

    with jax.named_scope("gate_up"):
        blocks = gate_up(side, lifted_order, near, far, lift_gain, gateup_weight, 768)
        gates, terms, ups = add_crossed(blocks[0], blocks[1:])
        activated = activate(gates, terms, ups, model, batches)
        activated = exchange(activated, "batch").reshape(total, hidden)

    with jax.named_scope("down_projection"):
        lowered = add_over_tensor(*spread_dot(targets, activated, down_weight))
        final = (residual + lowered).astype(jnp.bfloat16)
        layer_out = (
            final.reshape(share // both, STEPS, rows, width)
            .transpose(1, 0, 2, 3)
            .reshape(STEPS, share // STEPS, width)
        )
    return layer_out, cache_out, fresh_out


def solution(mesh):
    return jax.shard_map(
        on_device,
        mesh=mesh,
        in_specs=(
            P(None, None, "batch"),
            P("batch"),
            P("batch"),
            P("batch", "tensor"),
            P(None, "batch", "tensor"),
            P("tensor", "batch"),
            P(None, "batch", "tensor"),
            P("tensor", "batch"),
            P(None, "batch", None, "tensor"),
            P(),
        ),
        out_specs=(
            P(None, "tensor", "batch"),
            P(None, "batch", None, "tensor"),
            P(None, "batch", None, "tensor"),
        ),
        check_vma=False,
    )
```

```python
import functools
import math

import jax
import jax.numpy as jnp
import numpy as np
from jax import lax
from jax.experimental import pallas as pl
from jax.experimental.pallas import tpu as pltpu
from jax.sharding import PartitionSpec as P

HD = 128
LANES = 128
STEPS = 2
MIB = 1024 * 1024

rope_base = 1000000.0
norm_eps = 1e-05


def exchange(blocks, axis):
    return lax.all_to_all(blocks, axis, split_axis=0, concat_axis=0, tiled=True)


def after(value, earlier):
    return lax.optimization_barrier((value, earlier))[0]


def shift_along(block, minor_axis, count):
    side = math.isqrt(lax.axis_size("batch"))
    pairs = []
    for major in range(side):
        for minor in range(side):
            target = (
                (major, (minor + count) % side) if minor_axis else ((major + count) % side, minor)
            )
            pairs.append((major * side + minor, target[0] * side + target[1]))
    return lax.ppermute(block, "batch", pairs)


def shift_chips(block, count):
    size = lax.axis_size("tensor")
    return lax.ppermute(block, "tensor", [(at, (at + 2 * count) % size) for at in range(size)])


def swap_cores(block):
    size = lax.axis_size("tensor")
    return lax.ppermute(block, "tensor", [(at, at ^ 1) for at in range(size)])


def fold_kernel(count, *refs):
    sources, targets = refs[:count], refs[count:]
    terms = []
    for source in sources:
        terms += [source] if len(source.shape) == 2 else [source.at[at] for at in range(source.shape[0])]
    total = terms[0][...].astype(jnp.float32)
    for term in terms[1:]:
        total = total + term[...].astype(jnp.float32)
    rows = total.shape[0] // len(targets)
    for place, target in enumerate(targets):
        target[...] = total[place * rows : (place + 1) * rows].astype(target.dtype)


def fold(sources, pieces):
    rows, columns = sources[0].shape[-2:]
    kinds = [jnp.float32] + [jnp.bfloat16] * (pieces - 1)
    whole = pl.BlockSpec(memory_space=pltpu.VMEM)
    return pl.pallas_call(
        functools.partial(fold_kernel, len(sources)),
        out_shape=[jax.ShapeDtypeStruct((rows // pieces, columns), kind) for kind in kinds],
        in_specs=[whole] * len(sources),
        out_specs=[whole] * pieces,
        compiler_params=pltpu.CompilerParams(vmem_limit_bytes=32 * MIB),
        cost_estimate=pl.CostEstimate(flops=1, bytes_accessed=1, transcendentals=0),
        name="fold",
    )(*sources)


def exchange_minor(blocks):
    side = math.isqrt(lax.axis_size("batch"))
    groups = [[major * side + minor for minor in range(side)] for major in range(side)]
    return lax.all_to_all(
        blocks, "batch", split_axis=0, concat_axis=0, tiled=True, axis_index_groups=groups
    )


def exchange_minor(blocks):
    side = math.isqrt(lax.axis_size("batch"))
    groups = [[major * side + minor for minor in range(side)] for major in range(side)]
    return lax.all_to_all(
        blocks, "batch", split_axis=0, concat_axis=0, tiled=True, axis_index_groups=groups
    )


def add_along(own, terms):
    return functools.reduce(lambda total, term: total + term.astype(jnp.float32), terms, own)


def stack_kernel(*refs):
    sources, target = refs[:-1], refs[-1]
    total = sources[0][...].astype(jnp.float32)
    for source in sources[1:]:
        total = total + source[...].astype(jnp.float32)
    rows = target.shape[1]
    for place in range(target.shape[0]):
        target[place] = total[place * rows : (place + 1) * rows].astype(target.dtype)


def fold_stacked(sources):
    rows, columns = sources[0].shape
    shape = (len(sources), rows // len(sources), columns)
    whole = pl.BlockSpec(memory_space=pltpu.VMEM)
    return pl.pallas_call(
        stack_kernel,
        out_shape=jax.ShapeDtypeStruct(shape, jnp.bfloat16),
        in_specs=[whole] * len(sources),
        out_specs=whole,
        compiler_params=pltpu.CompilerParams(vmem_limit_bytes=32 * MIB),
        cost_estimate=pl.CostEstimate(flops=1, bytes_accessed=1, transcendentals=0),
        name="fold_stacked",
    )(*sources)


def activate_kernel(model, own_ref, *refs):
    terms, crossed_ref, out_ref = refs[:-2], refs[-2], refs[-1]
    hidden = out_ref.shape[2]
    gates = own_ref[...]
    for term in terms:
        gates = gates + term[...].astype(jnp.float32)
    ups = crossed_ref[0].astype(jnp.float32)
    for place in range(1, crossed_ref.shape[0]):
        ups = ups + crossed_ref[place].astype(jnp.float32)
    mean = (gates[:, hidden : hidden + 1] + gates[:, hidden + 1 : hidden + 2]) / model
    scale = lax.rsqrt(mean + norm_eps)
    gates, ups = gates[:, :hidden] * scale, ups * scale
    activated = (gates / (1.0 + jnp.exp(-gates)) * ups).astype(jnp.bfloat16)
    for copy in range(out_ref.shape[0]):
        out_ref[copy] = activated


def activate(own, terms, crossed, model, copies):
    _, rows, hidden = crossed.shape
    whole = pl.BlockSpec(memory_space=pltpu.VMEM)
    return pl.pallas_call(
        functools.partial(activate_kernel, model),
        out_shape=jax.ShapeDtypeStruct((copies, rows, hidden), jnp.bfloat16),
        in_specs=[whole] * (2 + len(terms)),
        out_specs=whole,
        compiler_params=pltpu.CompilerParams(vmem_limit_bytes=32 * MIB),
        cost_estimate=pl.CostEstimate(
            flops=8 * rows * hidden,
            bytes_accessed=2 * copies * rows * hidden,
            transcendentals=rows * hidden,
        ),
        name="activate",
    )(own, *terms, crossed)


def add_crossed(first, second):
    side = len(second)
    others = range(1, side)
    moved = [second[0]] + [shift_along(second[count], 0, count) for count in others]
    summed = fold([exchange_minor(first)], side)
    terms = [shift_along(summed[count], 0, count) for count in others]
    return summed[0], terms, exchange_minor(fold_stacked(moved))


def add_over_tensor(kept, sent):
    chips = lax.axis_size("tensor") // 2
    pieces = fold([kept, swap_cores(sent)], chips)
    total = pieces[0]
    for count in range(1, chips):
        total = total + shift_chips(pieces[count], count).astype(jnp.float32)
    return total


def blocks_along(values, side, place):
    rows = values.shape[0] // (side * side)
    return jnp.concatenate(
        [
            values[(major * side + place) * rows : (major * side + place + 1) * rows]
            for major in range(side)
        ],
        axis=0,
    )


def one_hot(index, count):
    places = lax.broadcasted_iota(jnp.int32, (index.shape[0], count), 1)
    return jnp.where(places == index, 1.0, 0.0).astype(jnp.bfloat16)


def dot(left, right):
    return jnp.dot(left, right, preferred_element_type=jnp.float32)


def split_pair(values):
    high = values.astype(jnp.bfloat16).astype(jnp.float32)
    return [high, values - high]


def in_lanes(columns):
    lanes = lax.broadcasted_iota(jnp.int32, (columns[0].shape[0], LANES), 1)
    packed = jnp.zeros(lanes.shape, jnp.float32)
    for place, value in enumerate(columns):
        packed = jnp.where(lanes == place, value, packed)
    return packed


def project_kernel(
    order_ref, parent_ref, input_ref, gain_ref, query_ref, keyval_ref, out_ref
):
    steps, count, width = input_ref.shape
    source = input_ref[...].reshape(steps * count, width)
    gain = gain_ref[...].astype(jnp.float32)
    order = order_ref[...]
    is_key = order < count
    own = dot(one_hot(order, steps * count), source)
    parents = dot(one_hot(parent_ref[...], count), input_ref[0]).astype(jnp.bfloat16)
    parents = dot(one_hot(jnp.where(is_key, order, order - count), count), parents)
    statistics = split_pair(jnp.sum(own * own, axis=1, keepdims=True)) + split_pair(
        jnp.sum(parents * parents, axis=1, keepdims=True)
    )
    own = (own * gain).astype(jnp.bfloat16)
    parents = (parents * gain).astype(jnp.bfloat16)
    values = jnp.concatenate(
        [
            dot(own, query_ref[...]),
            dot(own, keyval_ref[0]),
            dot(own, keyval_ref[1]),
            jnp.where(is_key, dot(parents, keyval_ref[0]), dot(parents, keyval_ref[1])),
            in_lanes(statistics),
        ],
        axis=1,
    ).astype(jnp.float32)
    blocks, held, _ = out_ref.shape
    rows = values.shape[0] // blocks
    for block in range(blocks):
        part = values[block * rows : (block + 1) * rows]
        for at in range(held // (2 * rows)):
            pair = [
                part[:, (2 * at + side) * LANES : (2 * at + side + 1) * LANES] for side in range(2)
            ]
            out_ref[block, 2 * at * rows : 2 * (at + 1) * rows] = jnp.concatenate(
                pair, axis=0
            ).astype(jnp.bfloat16)


def project_rows(batches, order, parents, layer_input, gain, query_weight, keyval_weight):
    total = order.shape[0]
    columns = query_weight.shape[1] + 3 * keyval_weight.shape[2] + LANES
    held = total // batches * columns // LANES
    whole = pl.BlockSpec(memory_space=pltpu.VMEM)
    return pl.pallas_call(
        project_kernel,
        out_shape=jax.ShapeDtypeStruct((batches, held, LANES), jnp.bfloat16),
        in_specs=[whole] * 6,
        out_specs=whole,
        compiler_params=pltpu.CompilerParams(vmem_limit_bytes=48 * MIB),
        cost_estimate=pl.CostEstimate(
            flops=2 * total * columns * gain.shape[0],
            bytes_accessed=2 * (gain.shape[0] + total) * columns,
            transcendentals=0,
        ),
        name="project_rows",
    )(order, parents, layer_input, gain.reshape(1, -1), query_weight, keyval_weight)


def gate_up_kernel(side, spans, order_ref, near_ref, far_ref, gain_ref, weight_ref, *refs):
    first_ref, second_refs = refs[0], refs[1 : 1 + side]
    held_ref, first_held, second_held, in_sems, first_sems, second_sems = refs[1 + side :]
    hidden = weight_ref.shape[2]
    loads = {}
    for half in (1, 0):
        for at, (start, size) in enumerate(spans):
            columns = pl.ds(start, size)
            loads[half, at] = pltpu.make_async_copy(
                weight_ref.at[half, :, columns],
                held_ref.at[half, :, columns],
                in_sems.at[half, at],
            )
    order = [(half, at) for half in (1, 0) for at in (range(len(spans)) if half else reversed(range(len(spans))))]
    ahead = 4
    for key in order[:ahead]:
        loads[key].start()

    def arrived(half, at):
        step = order.index((half, at))
        if step + ahead < len(order):
            loads[order[step + ahead]].start()
        loads[half, at].wait()

    lifted = jnp.concatenate([near_ref[...], far_ref[...]], axis=0)
    ordered = dot(one_hot(order_ref[...], lifted.shape[0]), lifted)
    plain = ordered * (1.0 / gain_ref[...].astype(jnp.float32))
    statistics = in_lanes(split_pair(jnp.sum(plain * plain, axis=1, keepdims=True)))
    ordered = ordered.astype(jnp.bfloat16)
    rows = ordered.shape[0] // side
    stores = []
    for at, (start, size) in enumerate(spans):
        arrived(1, at)
        ups = dot(ordered, held_ref[1, :, start : start + size])
        for place in range(side):
            second_held[place, :, start : start + size] = ups[
                place * rows : (place + 1) * rows
            ].astype(jnp.bfloat16)
    for place in range(side):
        stores.append(
            pltpu.make_async_copy(
                second_held.at[place], second_refs[place], second_sems.at[place]
            )
        )
        stores[-1].start()
    for at, (start, size) in reversed(list(enumerate(list(spans) + [(hidden, LANES)]))):
        if start < hidden:
            arrived(0, at)
            gates = dot(ordered, held_ref[0, :, start : start + size])
        else:
            gates = statistics
        for place in range(side):
            first_held[place, :, start : start + size] = blocks_along(gates, side, place).astype(
                jnp.bfloat16
            )
        columns = pl.ds(start, size)
        stores.append(
            pltpu.make_async_copy(
                first_held.at[:, :, columns], first_ref.at[:, :, columns], first_sems.at[at]
            )
        )
        stores[-1].start()
    for store in stores:
        store.wait()


def gate_up(side, order, near, far, gain, weight, tile):
    total, width = order.shape[0], near.shape[1]
    hidden = weight.shape[2]
    rows = total // side
    edges = [0] + list(range(hidden % tile or tile, hidden + 1, tile))
    spans = [(start, stop - start) for start, stop in zip(edges, edges[1:])]
    whole = pl.BlockSpec(memory_space=pltpu.VMEM)
    far_off = pl.BlockSpec(memory_space=pltpu.HBM)
    return pl.pallas_call(
        functools.partial(gate_up_kernel, side, spans),
        out_shape=[jax.ShapeDtypeStruct((side, rows, hidden + LANES), jnp.bfloat16)]
        + [jax.ShapeDtypeStruct((rows, hidden), jnp.bfloat16)] * side,
        in_specs=[whole] * 4 + [far_off],
        out_specs=[far_off] * (1 + side),
        scratch_shapes=[
            pltpu.VMEM(weight.shape, jnp.bfloat16),
            pltpu.VMEM((side, rows, hidden + LANES), jnp.bfloat16),
            pltpu.VMEM((side, rows, hidden), jnp.bfloat16),
            pltpu.SemaphoreType.DMA((2, len(spans))),
            pltpu.SemaphoreType.DMA((len(spans) + 1,)),
            pltpu.SemaphoreType.DMA((side,)),
        ],
        compiler_params=pltpu.CompilerParams(vmem_limit_bytes=58 * MIB),
        cost_estimate=pl.CostEstimate(
            flops=4 * total * width * hidden,
            bytes_accessed=4 * hidden * (width + total),
            transcendentals=0,
        ),
        name="gate_up",
    )(order, near, far, gain, weight)


def spread_dot_kernel(place_ref, rows_ref, weight_ref, kept_ref, sent_ref, total_ref):
    values = dot(rows_ref[...], weight_ref[...])
    blocks = place_ref.shape[0]
    rows = values.shape[0] // blocks
    for at in range(blocks):
        target = pl.ds(pl.multiple_of(place_ref[at], 8), rows)
        total_ref[target, :] = values[at * rows : (at + 1) * rows]
    half = kept_ref.shape[0]
    kept_ref[...] = total_ref[:half]
    sent_ref[...] = total_ref[half:].astype(jnp.bfloat16)


def spread_dot(places, values, weight):
    total, width = values.shape[0], weight.shape[1]
    whole = pl.BlockSpec(memory_space=pltpu.VMEM)
    return pl.pallas_call(
        spread_dot_kernel,
        out_shape=[
            jax.ShapeDtypeStruct((total // 2, width), kind) for kind in (jnp.float32, jnp.bfloat16)
        ],
        in_specs=[pl.BlockSpec(memory_space=pltpu.SMEM), whole, whole],
        out_specs=[whole] * 2,
        scratch_shapes=[pltpu.VMEM((total, width), jnp.float32)],
        compiler_params=pltpu.CompilerParams(vmem_limit_bytes=20 * MIB),
        cost_estimate=pl.CostEstimate(
            flops=2 * total * weight.size,
            bytes_accessed=2 * weight.size + 2 * total * (weight.shape[0] + 4 * width),
            transcendentals=0,
        ),
        name="spread_dot",
    )(places, values, weight)


def rotary(rows, first_position):
    inverse = np.exp(-math.log(rope_base) * np.arange(HD // 2, dtype=np.float64) * (2.0 / HD))
    angles = (first_position + np.repeat(np.arange(STEPS), rows))[:, None] * inverse[None, :]
    cosine, sine = np.cos(angles), np.sin(angles)
    return np.concatenate([cosine, cosine, -sine, sine], axis=1).astype(np.float32)


def attend_kernel(heads, rows, model, table_ref, cache_ref, *refs):
    out_ref, fresh_ref, kept_ref, query_ref, mix_ref, semaphores = refs
    total = STEPS * rows
    batches, span = kept_ref.shape[2:4]
    edge = (heads + 3) * HD
    stores = []
    for row in range(rows):
        for at in range(2):
            stores.append(
                pltpu.make_async_copy(
                    cache_ref.at[:, pl.ds((2 * (rows + row) + at) * span, span)],
                    kept_ref.at[at, row],
                    semaphores.at[at, row],
                )
            )
            stores[-1].start()
    parts = []
    for start in range(2 * total * span, cache_ref.shape[1], 2 * total):
        pair = cache_ref[0, start : start + 2 * total].astype(jnp.float32)
        for source in range(1, batches):
            pair = pair + cache_ref[source, start : start + 2 * total].astype(jnp.float32)
        parts += [pair[:total], pair[total:]]
    values = jnp.concatenate(parts, axis=1)
    cosine, sine = table_ref[:, :HD], table_ref[:, HD:]
    scale = lax.rsqrt((values[:, edge : edge + 1] + values[:, edge + 1 : edge + 2]) / model + norm_eps)
    parent_scale = lax.rsqrt(
        (values[:, edge + 2 : edge + 3] + values[:, edge + 3 : edge + 4]) / model + norm_eps
    )

    def rotate(block, cosine, sine):
        return block * cosine + pltpu.roll(block, HD // 2, 1) * sine

    def rounded(block):
        return block.astype(jnp.bfloat16).astype(jnp.float32)

    query_ref[...] = jnp.zeros(query_ref.shape, jnp.float32)
    for head in range(heads):
        block = values[:, head * HD : (head + 1) * HD] * scale
        query_ref[:, head, :] = rotate(block, cosine, sine)
    keys = rounded(rotate(values[:, heads * HD : (heads + 1) * HD] * scale, cosine, sine))
    news = rounded(values[:, (heads + 1) * HD : (heads + 2) * HD] * scale)
    parents = values[:, (heads + 2) * HD : edge] * parent_scale
    parent_keys = rounded(rotate(parents[:rows], cosine[:rows], sine[:rows]))
    parent_news = rounded(parents[rows:])
    fresh_ref[0] = jnp.concatenate([keys[:rows], parent_keys], axis=0)
    fresh_ref[1] = keys
    fresh_ref[2] = jnp.concatenate([news[:rows], parent_news], axis=0)
    fresh_ref[3] = news
    queries = query_ref[...].astype(jnp.bfloat16)
    wide = queries.astype(jnp.float32)
    scores = jnp.concatenate(
        [
            lax.dot_general(
                queries[row],
                cache_ref[:, 2 * row * span : (2 * row + 1) * span].reshape(-1, HD),
                (((1,), (1,)), ((), ())),
                preferred_element_type=jnp.float32,
            )
            for row in range(total)
        ],
        axis=0,
    ).reshape(total, queries.shape[1], -1) * (1.0 / math.sqrt(HD))
    extra = [
        jnp.sum(wide * fresh_ref[at][:, None, :], axis=2, keepdims=True) * (1.0 / math.sqrt(HD))
        for at in range(STEPS)
    ]
    later = lax.broadcasted_iota(jnp.int32, extra[1].shape, 0) >= rows
    extra[1] = jnp.where(later, extra[1], -jnp.inf)
    top = jnp.maximum(
        jnp.max(scores, axis=2, keepdims=True), jnp.maximum(extra[0], extra[1])
    )
    weights = jnp.exp(scores - top)
    extra = [jnp.exp(score - top) for score in extra]
    whole = jnp.sum(weights, axis=2, keepdims=True) + extra[0] + extra[1]
    weights = (weights / whole).astype(jnp.bfloat16)
    extra = [rounded(weight / whole) for weight in extra]
    for row in range(total):
        mix_ref[row] = dot(weights[row], cache_ref[:, (2 * row + 1) * span : (2 * row + 2) * span].reshape(-1, HD))
    mix_ref[...] = (
        mix_ref[...]
        + extra[0] * fresh_ref[2][:, None, :]
        + extra[1] * fresh_ref[3][:, None, :]
    )
    for head in range(heads):
        block = mix_ref[:, head, :].astype(jnp.bfloat16)
        for copy in range(out_ref.shape[0]):
            out_ref[copy, :, head * HD : (head + 1) * HD] = block
    for store in stores:
        store.wait()


def attend(returned, heads, rows, past, model):
    batches, total = returned.shape[0], STEPS * rows
    padded = -(-heads // 8) * 8
    whole = pl.BlockSpec(memory_space=pltpu.VMEM)
    return pl.pallas_call(
        functools.partial(attend_kernel, heads, rows, model),
        out_shape=[
            jax.ShapeDtypeStruct((batches, total, heads * HD), jnp.bfloat16),
            jax.ShapeDtypeStruct((2 * STEPS, total, HD), jnp.float32),
            jax.ShapeDtypeStruct((2, rows, batches, past // batches, HD), jnp.bfloat16),
        ],
        grid=(1,),
        in_specs=[whole, pl.BlockSpec(returned.shape, lambda step: (0, 0, 0))],
        out_specs=[whole] * 2 + [pl.BlockSpec(memory_space=pl.ANY)],
        scratch_shapes=[pltpu.VMEM((total, padded, HD), jnp.float32)] * 2
        + [pltpu.SemaphoreType.DMA((2, rows))],
        compiler_params=pltpu.CompilerParams(vmem_limit_bytes=48 * MIB),
        cost_estimate=pl.CostEstimate(
            flops=4 * total * padded * past * HD,
            bytes_accessed=4 * returned.size,
            transcendentals=total * padded * past,
        ),
        name="attend",
    )(jnp.asarray(rotary(rows, past)), returned)


def cut_kernel(cache_ref, out_ref):
    blocks, rows, halves, span, _ = out_ref.shape
    for block in range(blocks):
        for half in range(halves):
            out_ref[block, :, half] = cache_ref[half, :, block * span : (block + 1) * span]


def cut_positions(cache, blocks):
    halves, rows, past, width = cache.shape
    shape = (blocks, rows, halves, past // blocks, width)
    whole = pl.BlockSpec(memory_space=pltpu.VMEM)
    return pl.pallas_call(
        cut_kernel,
        out_shape=jax.ShapeDtypeStruct(shape, cache.dtype),
        in_specs=[whole],
        out_specs=whole,
        compiler_params=pltpu.CompilerParams(vmem_limit_bytes=58 * MIB),
        cost_estimate=pl.CostEstimate(
            flops=0, bytes_accessed=4 * cache.size, transcendentals=0
        ),
        name="cut_positions",
    )(cache)


def pick_kernel(index_ref, table_ref, sum_ref, out_ref):
    span = table_ref.shape[1]
    count = index_ref.shape[0] // out_ref.shape[0]

    @pl.loop(0, out_ref.shape[0])
    def _(block):
        for row in range(count):
            out_ref[block, row * span : (row + 1) * span] = table_ref[
                index_ref[block * count + row]
            ]
        out_ref[block, count * span :] = sum_ref[block]


def pick_rows(table, index, sums):
    batches, held, _ = sums.shape
    count = index.shape[0] // batches * table.shape[1]
    whole = pl.BlockSpec(memory_space=pltpu.VMEM)
    return pl.pallas_call(
        pick_kernel,
        out_shape=jax.ShapeDtypeStruct((batches, count + held, LANES), table.dtype),
        in_specs=[pl.BlockSpec(memory_space=pltpu.SMEM), whole, whole],
        out_specs=whole,
        compiler_params=pltpu.CompilerParams(vmem_limit_bytes=32 * MIB),
        cost_estimate=pl.CostEstimate(
            flops=0, bytes_accessed=4 * batches * (count + held) * LANES, transcendentals=0
        ),
        name="pick_rows",
    )(index, table, sums)


def on_device(
    layer_input,
    attn_gain,
    ffn_gain,
    query_weight,
    keyval_weight,
    output_weight,
    gateup_weight,
    down_weight,
    past_cache,
    parent_rows,
):
    batches = lax.axis_size("batch")
    tensors = lax.axis_size("tensor")
    side = math.isqrt(batches)
    chips = tensors // 2
    batch_index = lax.axis_index("batch")
    tensor_index = lax.axis_index("tensor")
    my_major = batch_index // side
    my_chip, my_core = tensor_index // 2, tensor_index % 2
    _, rows, past, kv_width = past_cache.shape
    width = layer_input.shape[2]
    model = width * batches
    head_width = query_weight.shape[1]
    heads = head_width // HD
    hidden = gateup_weight.shape[2]
    both = STEPS * rows
    total = batches * both
    share = total // tensors
    span = past // batches

    with jax.named_scope("cache_spread"):
        pieces = cut_positions(past_cache, batches)
        spread = exchange(pieces, "batch").reshape(batches * rows, 2 * span, kv_width)

    with jax.named_scope("places"):
        parents = parent_rows.reshape(STEPS, batches, rows)
        origin = jnp.take(parent_rows[0], parent_rows[1], axis=0)
        wanted = jnp.stack([parents[0], origin.reshape(batches, rows)], axis=1).reshape(total)
        place = jnp.arange(total, dtype=jnp.int32)
        inner = place % both
        near = place // both
        input_order = ((inner // rows) * (batches * rows) + near * rows + inner % rows)[:, None]
        row = (my_major + place // (side * both)) % side * side + place // both % side
        row = row * both + inner
        owner = row // share
        lifted_order = (owner % 2 != my_core).astype(jnp.int32) * (total // 2)
        lifted_order = lifted_order + (my_chip - owner // 2 + chips) % chips * share
        lifted_order = (lifted_order + row % share)[:, None]
        block = jnp.arange(batches, dtype=jnp.int32)
        owner = block * both // share
        targets = (owner % 2 != my_core).astype(jnp.int32) * (total // 2)
        targets = targets + (owner // 2 - my_chip + chips) % chips * share
        targets = targets + block * both % share

    with jax.named_scope("project"):
        sums = project_rows(
            batches,
            input_order,
            parent_rows[1][:, None],
            after(layer_input, pieces),
            attn_gain,
            query_weight,
            keyval_weight,
        )

    with jax.named_scope("cache_return"):
        lift_gain = ffn_gain.reshape(1, -1)
        ready = after(wanted, (lifted_order, targets, lift_gain))
        returned = exchange(pick_rows(spread, ready, sums), "batch")

    with jax.named_scope("attention"):
        attended, fresh, kept = attend(returned, heads, rows, past, model)
        fresh_out = fresh.reshape(2, STEPS, both, kv_width)[:, :, rows:].transpose(0, 2, 1, 3)
        fresh_out = fresh_out.astype(jnp.bfloat16)
        cache_out = kept.reshape(2, rows, past, kv_width)
        attended = exchange(attended, "batch").reshape(total, head_width)

    with jax.named_scope("output_projection"):
        own_inputs = lax.dynamic_slice_in_dim(
            layer_input, tensor_index * (share // STEPS), share // STEPS, 1
        )
        own_inputs = (
            own_inputs.reshape(STEPS, share // both, rows, width)
            .transpose(1, 0, 2, 3)
            .reshape(share, width)
        )
        mixed = add_over_tensor(*spread_dot(targets, attended, output_weight))
        residual = own_inputs.astype(jnp.float32) + mixed
        lifted = (residual * ffn_gain.astype(jnp.float32)).astype(jnp.bfloat16)
        near = jnp.concatenate(
            [lifted] + [shift_chips(lifted, count) for count in range(1, chips)], axis=0
        )
        far = swap_cores(near)

    with jax.named_scope("gate_up"):
        blocks = gate_up(side, lifted_order, near, far, lift_gain, gateup_weight, 1280)
        gates, terms, ups = add_crossed(blocks[0], blocks[1:])
        activated = activate(gates, terms, ups, model, batches)
        activated = exchange(activated, "batch").reshape(total, hidden)

    with jax.named_scope("down_projection"):
        lowered = add_over_tensor(*spread_dot(targets, activated, down_weight))
        final = (residual + lowered).astype(jnp.bfloat16)
        layer_out = (
            final.reshape(share // both, STEPS, rows, width)
            .transpose(1, 0, 2, 3)
            .reshape(STEPS, share // STEPS, width)
        )
    return layer_out, cache_out, fresh_out


def solution(mesh):
    return jax.shard_map(
        on_device,
        mesh=mesh,
        in_specs=(
            P(None, None, "batch"),
            P("batch"),
            P("batch"),
            P("batch", "tensor"),
            P(None, "batch", "tensor"),
            P("tensor", "batch"),
            P(None, "batch", "tensor"),
            P("tensor", "batch"),
            P(None, "batch", None, "tensor"),
            P(),
        ),
        out_specs=(
            P(None, "tensor", "batch"),
            P(None, "batch", None, "tensor"),
            P(None, "batch", None, "tensor"),
        ),
        check_vma=False,
    )
```
